32 devices in a mesh: req: 16 (over z, y, core), tp: 2 (over x).
Axes of the slice: x: 2, y: 2, z: 4, core: 2. Of those that a mesh axis runs over, the one named last changes fastest.
Arguments:
- states: bfloat16 [4096, 3072], P('req', 'tp'), may hold values from -12 to 12
- query_weight: bfloat16 [3072, 1536], P(None, 'tp'), may hold values from -0.75 to 0.75
- key_value_weight: bfloat16 [3072, 512], P(None, 'tp'), may hold values from -0.75 to 0.75
- lengths: int32 [16], P('req'), may hold values from 1 to 256, 2048 in all
- adapter_ids: int32 [16], P('req'), may hold values from 0 to 63, as said below
- adapter_slot: int32 [64], replicated, may hold values from 0 to 63, as said below
- down_store: bfloat16 [64, 3072, 32], P('req', 'tp'), may hold values from -0.109375 to 0.109375
- query_up_store: bfloat16 [64, 16, 1536], P('req', None, 'tp'), may hold values from -1.5 to 1.5
- key_value_store: bfloat16 [64, 16, 512], P('req', None, 'tp'), may hold values from -1.5 to 1.5
Outputs:
- context: bfloat16 [4096, 1536], P('req', 'tp')
The draws below stay inside these ranges and needn't reach their ends.
Inputs may be any that keep to these rules, and one draw needn't show every extreme that they name: `adapter_ids`: exactly 16 distinct adapters are named among all 16 requests. `adapter_slot`: distinct adapters have distinct rows.
All inputs are finite; a program needn't handle non-finite values. No bound on the sum of `lengths` on one device may be relied on, other than what follows from the above.
Results may differ from the reference program's by a relative error of at most 0.0072.
Values may be sent and summed in bfloat16 or wider, within the bound.
A program may use at most 64 MiB of HBM per device.

```python
import math
import jax
import jax.numpy as jnp
import numpy as np
from jax import lax

D = 3072
HEADS = 12
KV_HEADS = 2
HEAD_DIM = 128
ADAPTER_RANK = 16
ADAPTERS = 64
ACTIVE = 16
SLOT = 256
REQS = 16
TOKENS = 4096
ADP_SLOTS = 64


def draw_states(key, part):
    first_key = jax.random.fold_in(key, 1)
    result = jnp.clip(jax.random.normal(first_key, (TOKENS, D), jnp.float32), -6.0, 6.0)
    return result.astype(jnp.bfloat16)


def draw_query_weight(key, part):
    independent = jax.random.normal(jax.random.fold_in(key, 12), (D, HEADS * HEAD_DIM), jnp.float32) / math.sqrt(D)
    result = independent
    return jnp.clip(result, -0.75, 0.75).astype(jnp.bfloat16)


def draw_key_value_weight(key, part):
    independent = jax.random.normal(jax.random.fold_in(key, 13), (D, 2 * KV_HEADS * HEAD_DIM), jnp.float32) / math.sqrt(D)
    result = independent
    return jnp.clip(result, -0.75, 0.75).astype(jnp.bfloat16)


def draw_adapter_ids(key, part):
    selected_adapters = jax.random.permutation(jax.random.fold_in(key, 21), ADAPTERS)[:ACTIVE]
    first_pick = jax.random.randint(jax.random.fold_in(key, 22), (REQS,), 0, ACTIVE)
    second_pick = jax.random.randint(jax.random.fold_in(key, 23), (REQS,), 0, ACTIVE)
    picks = jnp.minimum(first_pick, second_pick)
    ranks = jnp.arange(REQS)
    picks = jnp.where(ranks < ACTIVE, ranks, picks)
    picks = picks[jax.random.permutation(jax.random.fold_in(key, 24), REQS)]
    return selected_adapters[picks].astype(jnp.int32)


def draw_adapter_slot(key, part):
    return jax.random.permutation(jax.random.fold_in(key, 31), ADP_SLOTS)[:ADAPTERS].astype(jnp.int32)


def shard_levels(rng, shape, cuts, smallest, top_value):
    loudness = 1.0
    for dim, parts in cuts:
        steps = jax.random.uniform(jax.random.fold_in(jax.random.fold_in(rng, 6), dim), (parts,), jnp.float32, smallest / len(cuts), top_value / len(cuts))
        loudness = loudness * jnp.repeat(jnp.exp(steps), shape[dim] // parts).reshape((-1,) + (1,) * (len(shape) - 1 - dim))
    return loudness


def profile(count, total, limit, lean):
    weights = [(1 << 20) // math.isqrt(grade ** lean) + 1 for grade in range(2, count + 1)]
    rest, given = total - limit - (count - 1), [1] * (count - 1)
    while rest > 0:
        free = [i for i in range(count - 1) if given[i] < limit]
        mass, budget = sum([weights[i] for i in free]), rest
        for i in free:
            extra = min(limit - given[i], max(1, budget * weights[i] // mass), rest)
            given[i] = given[i] + extra
            rest = rest - extra
    return np.array([limit] + given)


def ragged(own_key, number_of, total, reach, lean):
    if number_of == 2:
        one = jax.random.randint(own_key, (), max(1, total - reach), min(reach, total - 1) + 1)
        return jnp.stack([one, total - one])
    tallies = jnp.asarray(profile(number_of, total, reach, lean), jnp.int32)
    twos = (number_of - 1) // 2
    source_of, taker = tallies[1:1 + 2 * twos:2], tallies[2:2 + 2 * twos:2]
    margin = jnp.minimum(source_of - 1, reach - taker)
    shifted = jax.random.randint(jax.random.fold_in(own_key, 1), (twos,), 0, 1 << 20) % (margin + 1)
    tallies = tallies.at[1:1 + 2 * twos:2].set(source_of - shifted).at[2:2 + 2 * twos:2].set(taker + shifted)
    return tallies[jax.random.permutation(jax.random.fold_in(own_key, 2), number_of)]


def noise(own_key, dims, width, most, shards=(), held_as=jnp.bfloat16):
    drawn = width * jax.random.normal(own_key, dims, jnp.float32)
    if shards:
        drawn = drawn * shard_levels(own_key, dims, shards, -0.22, 0.18)
    return jnp.clip(drawn, -most, most).astype(held_as)


def setup_inputs(seed: int = 0) -> dict:
    splits = jax.random.split(jax.random.key(seed), 10)
    return {
        "states": draw_states(jax.random.fold_in(splits[9], 71), 0),
        "query_weight": draw_query_weight(jax.random.fold_in(splits[9], 71), 0),
        "key_value_weight": draw_key_value_weight(jax.random.fold_in(splits[9], 71), 0),
        "lengths": ragged(splits[3], REQS, REQS * SLOT // 2, SLOT, 2).astype(jnp.int32),
        "adapter_ids": draw_adapter_ids(jax.random.fold_in(splits[9], 71), 0),
        "adapter_slot": draw_adapter_slot(jax.random.fold_in(splits[9], 71), 0),
        "down_store": noise(splits[6], (ADP_SLOTS, D, 2 * ADAPTER_RANK), D ** -0.5, 0.109375, ((0, 16), (1, 2))),
        "query_up_store": noise(splits[7], (ADP_SLOTS, ADAPTER_RANK, HEADS * HEAD_DIM), ADAPTER_RANK ** -0.5, 1.5, ((0, 16), (2, 2))),
        "key_value_store": noise(splits[8], (ADP_SLOTS, ADAPTER_RANK, 2 * KV_HEADS * HEAD_DIM), ADAPTER_RANK ** -0.5, 1.5, ((0, 16), (2, 2))),
    }


adapter_scale = 0.5
rope_base = 100000000000.0

def rotate(field):
    half = field.shape[-1] // 2
    count = field.shape[-3]
    position = jnp.arange(count).astype(jnp.float32)
    inverse = rope_base ** (-(jnp.arange(half).astype(jnp.float32) * 2.0) / field.shape[-1])
    angle = position[:, None] * inverse[None, :]
    cosine = jnp.cos(angle)[:, None, :]
    sine = jnp.sin(angle)[:, None, :]
    first_half = field[..., :half]
    second_half = field[..., half:]
    return jnp.concatenate([first_half * cosine - second_half * sine, second_half * cosine + first_half * sine], axis=-1)

def reference(states, query_weight, key_value_weight, lengths, adapter_ids, adapter_slot, down_store, query_up_store, key_value_store):
    group = HEADS // KV_HEADS
    key_width = KV_HEADS * HEAD_DIM
    scale = 1.0 / math.sqrt(HEAD_DIM)
    slots = adapter_slot[adapter_ids].astype(jnp.int32)
    blocks = states.reshape(REQS, SLOT, D)

    def one_request(item):
        token_states, selected_adapters, length = item
        rank_middle = jnp.dot(token_states, down_store[selected_adapters], preferred_element_type=jnp.float32).astype(jnp.bfloat16)
        query_plain = jnp.dot(token_states, query_weight, preferred_element_type=jnp.float32) + adapter_scale * jnp.dot(rank_middle[:, :ADAPTER_RANK], query_up_store[selected_adapters], preferred_element_type=jnp.float32)
        key_value_pair = (jnp.dot(token_states, key_value_weight, preferred_element_type=jnp.float32) + adapter_scale * jnp.dot(rank_middle[:, ADAPTER_RANK:], key_value_store[selected_adapters], preferred_element_type=jnp.float32)).astype(jnp.bfloat16)
        queries = rotate(query_plain.reshape(SLOT, HEADS, HEAD_DIM)).astype(jnp.bfloat16)
        keys = rotate(key_value_pair[:, :key_width].astype(jnp.float32).reshape(SLOT, KV_HEADS, HEAD_DIM)).astype(jnp.bfloat16)
        values = key_value_pair[:, key_width:].reshape(SLOT, KV_HEADS, HEAD_DIM)
        keys = jnp.repeat(keys, group, axis=1)
        values = jnp.repeat(values, group, axis=1)
        scores = jnp.einsum('qhd,khd->hqk', queries.astype(jnp.float32), keys.astype(jnp.float32)) * scale
        position = jnp.arange(SLOT, dtype=jnp.int32)
        allowed = (position[None, :] <= position[:, None]) & (position[None, :] < length)
        scores = jnp.where(allowed[None, :, :], scores, -jnp.inf)
        highest = lax.optimization_barrier(jnp.max(scores, axis=-1, keepdims=True))
        expo = jnp.exp(scores - highest)
        weights = (expo / lax.optimization_barrier(jnp.sum(expo, axis=-1, keepdims=True))).astype(jnp.bfloat16)
        context = jnp.einsum('hqk,khd->qhd', weights.astype(jnp.float32), values.astype(jnp.float32))
        context = jnp.where((position < length)[:, None, None], context, 0.0)
        return context.reshape(SLOT, HEADS * HEAD_DIM).astype(jnp.bfloat16)
    result = lax.map(one_request, (blocks, slots, lengths))
    return result.reshape(TOKENS, HEADS * HEAD_DIM)
```

```python
import functools
import math

import jax
import jax.numpy as jnp
import numpy as np
from jax import lax
from jax.experimental import pallas as pl
from jax.experimental.pallas import tpu as pltpu
from jax.sharding import PartitionSpec as P

HEADS = 12
HEAD_DIM = 128


adapter_scale = 0.5
rope_base = 100000000000.0


def rotate(field):
    half = field.shape[-1] // 2
    count = field.shape[-3]
    position = jnp.arange(count).astype(jnp.float32)
    inverse = rope_base ** (-(jnp.arange(half).astype(jnp.float32) * 2.0) / field.shape[-1])
    angle = position[:, None] * inverse[None, :]
    cosine = jnp.cos(angle)[:, None, :]
    sine = jnp.sin(angle)[:, None, :]
    first_half = field[..., :half]
    second_half = field[..., half:]
    return jnp.concatenate(
        [first_half * cosine - second_half * sine, second_half * cosine + first_half * sine],
        axis=-1,
    )


def lookup_slots(wanted, adapter_slot):
    table = jnp.arange(adapter_slot.shape[0], dtype=jnp.int32)
    matches = wanted[:, None] == table[None, :]
    return jnp.sum(jnp.where(matches, adapter_slot[None, :], 0), axis=1)


def local(
    states,
    query_weight,
    key_value_weight,
    lengths,
    adapter_ids,
    adapter_slot,
    down_store,
    query_up_store,
    key_value_store,
):
    tp_index = lax.axis_index("tp")
    req_dev = lengths.shape[0]
    rows_total = states.shape[0]
    slot_len = rows_total // req_dev
    q_cols = query_weight.shape[1]
    kv_cols = key_value_weight.shape[1]
    heads_here = q_cols // HEAD_DIM
    pooled = (
        lax.all_gather(down_store, "req", axis=0, tiled=True),
        lax.all_gather(query_up_store, "req", axis=0, tiled=True),
        lax.all_gather(key_value_store, "req", axis=0, tiled=True),
    )
    own_slots = lookup_slots(adapter_ids, adapter_slot)
    adapter_down, adapter_query, adapter_pair = (
        jnp.take(member, own_slots, axis=0) for member in pooled
    )
    full_down = lax.all_gather(adapter_down, "tp", axis=1, tiled=True)
    piece = lax.all_gather(states, "tp", axis=1, tiled=True)
    width = piece.shape[1]
    grouped = piece.reshape(req_dev, slot_len, width)
    query_total = jnp.dot(piece, query_weight, preferred_element_type=jnp.float32)
    key_value_sum = jnp.dot(piece, key_value_weight, preferred_element_type=jnp.float32)
    rank_sum = jnp.einsum("rsd,rdk->rsk", grouped, full_down, preferred_element_type=jnp.float32)
    rank_mid = rank_sum.astype(jnp.bfloat16)
    rank_cols = rank_mid.shape[2] // 2
    query_addition = jnp.einsum(
        "rsk,rkc->rsc",
        rank_mid[:, :, :rank_cols],
        adapter_query,
        preferred_element_type=jnp.float32,
    ).reshape(rows_total, q_cols)
    key_value_extra = jnp.einsum(
        "rsk,rkc->rsc", rank_mid[:, :, rank_cols:], adapter_pair, preferred_element_type=jnp.float32
    ).reshape(rows_total, kv_cols)
    query_plain = query_total + adapter_scale * query_addition
    key_value_own = (key_value_sum + adapter_scale * key_value_extra).astype(jnp.bfloat16)
    pair_all = lax.all_gather(key_value_own, "tp", axis=1, tiled=True)
    key_width = pair_all.shape[1] // 2
    kv_heads = key_width // HEAD_DIM
    group = HEADS // kv_heads
    kv_index = tp_index * heads_here // group
    key_block = lax.dynamic_slice_in_dim(pair_all, kv_index * HEAD_DIM, HEAD_DIM, 1)
    value_block = lax.dynamic_slice_in_dim(pair_all, key_width + kv_index * HEAD_DIM, HEAD_DIM, 1)
    queries = rotate(query_plain.reshape(req_dev, slot_len, heads_here, HEAD_DIM)).astype(
        jnp.bfloat16
    )
    keys_one = rotate(key_block.astype(jnp.float32).reshape(req_dev, slot_len, 1, HEAD_DIM)).astype(
        jnp.bfloat16
    )[:, :, 0, :]
    values_one = value_block.reshape(req_dev, slot_len, HEAD_DIM)
    scale = 1.0 / math.sqrt(HEAD_DIM)
    scores = (
        jnp.einsum("rqhd,rkd->rhqk", queries, keys_one, preferred_element_type=jnp.float32) * scale
    )
    position = jnp.arange(slot_len, dtype=jnp.int32)
    allowed = (position[None, None, :] <= position[None, :, None]) & (
        position[None, None, :] < lengths[:, None, None]
    )
    scores = jnp.where(allowed[:, None, :, :], scores, -jnp.inf)
    highest = jnp.max(scores, axis=-1, keepdims=True)
    expo = jnp.exp(scores - highest)
    weights = (expo / jnp.sum(expo, axis=-1, keepdims=True)).astype(jnp.bfloat16)
    context = jnp.einsum("rhqk,rkd->rqhd", weights, values_one, preferred_element_type=jnp.float32)
    live_rows = position[None, :] < lengths[:, None]
    context = jnp.where(live_rows[:, :, None, None], context, 0.0)
    return context.reshape(rows_total, q_cols).astype(jnp.bfloat16)


MESH = pl.DeviceIdType.MESH
PIECES = 4
GROUPS = ((0, 192), (192, 64))


def fused(
    planes,
    ids,
    slots,
    lengths,
    states,
    wq,
    wkv,
    rows,
    cosine,
    sine,
    out,
    own_st,
    other_st,
    w_own,
    w_other,
    total,
    plane,
    ids_own,
    ids_in,
    leaving,
    landed,
    down,
    ups,
    mid_out,
    mid_in,
    kv_own,
    kv_in,
    local_sem,
    st_send,
    st_recv,
    y_send,
    y_recv,
    c_send,
    c_recv,
    f_send,
    f_recv,
    i_send,
    i_recv,
    z_send,
    z_recv,
    m_send,
    m_recv,
    kv_send,
    kv_recv,
):
    r = lax.axis_index("req")
    tp = lax.axis_index("tp")
    per_plane = 4
    count = planes * per_plane
    half = own_st.shape[1]
    q_cols = wq.shape[1]
    tokens = own_st.shape[0]
    step = tokens // PIECES
    mine = rows.shape[1]
    core_peer = r + 1 - 2 * (r % 2)
    y_peer = r + 2 - 4 * ((r // 2) % 2)
    z_peers = [(r + per_plane * d) % count for d in range(1, planes)]
    across = 1 - tp
    base = (r // per_plane) * (per_plane * mine)

    def place(index):
        return pl.ds((index % per_plane) * mine, mine)

    def remote(src, dst, send, recv, who):
        return pltpu.make_async_remote_copy(
            src_ref=src, dst_ref=dst, send_sem=send, recv_sem=recv, device_id=who, device_id_type=MESH
        )

    own_rows = pl.ds(pl.multiple_of(tp * half, half), half)
    other_rows = pl.ds(pl.multiple_of(across * half, half), half)
    loads = [
        pltpu.make_async_copy(states, own_st, local_sem.at[0]),
        pltpu.make_async_copy(wq.at[own_rows], w_own.at[:, :q_cols], local_sem.at[1]),
        pltpu.make_async_copy(wkv.at[own_rows], w_own.at[:, q_cols:], local_sem.at[2]),
        pltpu.make_async_copy(wq.at[other_rows], w_other.at[:, :q_cols], local_sem.at[3]),
        pltpu.make_async_copy(wkv.at[other_rows], w_other.at[:, q_cols:], local_sem.at[4]),
        pltpu.make_async_copy(rows, plane.at[:, place(r)], local_sem.at[5]),
    ]
    for copy in loads:
        copy.start()

    ids_own[...] = jnp.full(ids_own.shape, slots[ids[0]], jnp.int32)

    barrier = pltpu.get_barrier_semaphore()
    for peer in [core_peer, y_peer] + z_peers:
        pl.semaphore_signal(barrier, inc=1, device_id={"req": peer}, device_id_type=MESH)
    pl.semaphore_signal(barrier, inc=1, device_id={"tp": across}, device_id_type=MESH)
    pl.semaphore_wait(barrier, planes + 2)

    id_copies = [
        remote(ids_own, ids_in.at[d], i_send.at[d], i_recv.at[d], {"req": peer})
        for d, peer in enumerate(z_peers)
    ]
    st_copies = [
        remote(
            states.at[pl.ds(p * step, step)],
            other_st.at[pl.ds(p * step, step)],
            st_send.at[p],
            st_recv.at[p],
            {"tp": across},
        )
        for p in range(PIECES)
    ]
    y_copies = [
        remote(rows.at[k], plane.at[k, place(r)], y_send.at[k], y_recv.at[k], {"req": y_peer})
        for k in range(4)
    ]
    c_copies = [
        remote(rows.at[k], plane.at[k, place(r)], c_send.at[k], c_recv.at[k], {"req": core_peer})
        for k in range(4)
    ]
    f_copies = [
        remote(
            plane.at[k, place(y_peer)],
            plane.at[k, place(y_peer)],
            f_send.at[k],
            f_recv.at[k],
            {"req": core_peer},
        )
        for k in range(4)
    ]
    for copy in id_copies:
        copy.start()
    for k in range(4):
        st_copies[k].start()
        y_copies[k].start()
        c_copies[k].start()

    for n in (0, 1, 2):
        loads[n].wait()
    total[...] = jnp.dot(own_st[...], w_own[...], preferred_element_type=jnp.float32)
    loads[5].wait()
    for copy in id_copies:
        copy.wait_recv()
    loads[3].wait()
    loads[4].wait()

    def add_piece(p):
        st_copies[p].wait_recv()
        span = pl.ds(p * step, step)
        total[span] += jnp.dot(other_st[span], w_other[...], preferred_element_type=jnp.float32)

    z_copies = []
    selves = []
    for k in range(4):
        y_copies[k].wait_recv()
        f_copies[k].start()
        c_copies[k].wait_recv()
        f_copies[k].wait_recv()

        def pick(j, sums, k=k):
            record = plane[k, j]
            made = []
            for d in range(planes):
                wanted = ids_own[...] if d == 0 else ids_in[planes - 1 - d]
                flag = jnp.where(wanted == base + j, 1.0, 0.0).astype(jnp.bfloat16)
                flag = jnp.concatenate([flag] * (record.shape[1] // flag.shape[1]), axis=1)
                made.append(sums[d] + flag * record)
            return tuple(made)

        zero = jnp.zeros(plane.shape[2:], jnp.bfloat16)
        sums = lax.fori_loop(0, per_plane * mine, pick, (zero,) * planes)
        for d in range(1, planes):
            leaving[k, d - 1] = sums[d]
        ups[k] = sums[0]
        sent = [
            remote(
                leaving.at[k, d],
                landed.at[k, d],
                z_send.at[k, d],
                z_recv.at[k, d],
                {"req": peer},
            )
            for d, peer in enumerate(z_peers)
        ]
        for copy in sent:
            copy.start()
        z_copies.append(sent)
        if k in (1, 3):
            add_piece(k // 2)

    def take(k):
        for copy in z_copies[k]:
            copy.wait_recv()
        record = ups[k]
        for d in range(planes - 1):
            record = record + landed[k, d]
        return record

    rank = down.shape[0] // 2
    wide = plane.shape[3]
    left = half - wide
    down[0:rank, 0:wide] = take(0)
    down[rank:, 0:wide] = take(1)
    tail = take(2)
    down[0:rank, wide:] = tail[:, :left]
    down[rank:, wide:] = tail[:, left:]
    mid_out[...] = lax.dot_general(
        down[...], own_st[...], (((1,), (1,)), ((), ())), preferred_element_type=jnp.float32
    )
    mid_copy = remote(mid_out, mid_in, m_send.at[0], m_recv.at[0], {"tp": across})
    mid_copy.start()
    up = take(3)
    col = lax.broadcasted_iota(jnp.int32, (rank, wide), 1)
    empty = jnp.zeros_like(up)
    lifted = jnp.concatenate([jnp.where(col < q_cols, up, empty), jnp.where(col < q_cols, empty, up)], axis=0)
    add_piece(2)
    mid_copy.wait_recv()
    mid = jnp.transpose(mid_out[...] + mid_in[...]).astype(jnp.bfloat16)
    extra = 0.5 * jnp.dot(mid, lifted, preferred_element_type=jnp.float32)
    total[...] += extra

    kv_copies = []
    keep = pl.ds(pl.multiple_of(tp * HEAD_DIM, HEAD_DIM), HEAD_DIM)
    give = pl.ds(pl.multiple_of(across * HEAD_DIM, HEAD_DIM), HEAD_DIM)
    for g, (first, size) in enumerate(GROUPS):
        if g == 1:
            add_piece(3)
        span = pl.ds(first, size)
        kv_own[span] = total[span, q_cols:].astype(jnp.bfloat16)
        copy = remote(
            kv_own.at[span, give], kv_in.at[span], kv_send.at[g], kv_recv.at[g], {"tp": across}
        )
        copy.start()
        kv_copies.append(copy)

    scale = 1.0 / math.sqrt(HEAD_DIM)
    length = lengths[0]

    def turn(x, span):
        return (x * cosine[span] + pltpu.roll(x, HEAD_DIM // 2, 1) * sine[span]).astype(jnp.bfloat16)

    key_parts = []
    value_parts = []
    for g, (first, size) in enumerate(GROUPS):
        span = pl.ds(first, size)
        turned = [
            turn(total[span, h * HEAD_DIM : (h + 1) * HEAD_DIM], span)
            for h in range(q_cols // HEAD_DIM)
        ]
        kv_copies[g].wait_recv()
        kept = kv_own[span, keep]
        came = kv_in[span]
        first_side = jnp.full(kept.shape, tp, jnp.int32) == 0
        key = jnp.where(first_side, kept.astype(jnp.float32), came.astype(jnp.float32))
        value = jnp.where(first_side, came.astype(jnp.float32), kept.astype(jnp.float32))
        key_parts.append(turn(key, span))
        value_parts.append(value.astype(jnp.bfloat16))
        reach = first + size
        keys = jnp.concatenate(key_parts, axis=0) if g else key_parts[0]
        values = jnp.concatenate(value_parts, axis=0) if g else value_parts[0]
        row = lax.broadcasted_iota(jnp.int32, (size, reach), 0) + first
        column = lax.broadcasted_iota(jnp.int32, (size, reach), 1)
        allowed = (column <= row) & (column < length)
        live = lax.broadcasted_iota(jnp.int32, (size, HEAD_DIM), 0) + first < length
        for h, query in enumerate(turned):
            scores = lax.dot_general(
                query, keys, (((1,), (1,)), ((), ())), preferred_element_type=jnp.float32
            )
            scores = jnp.where(allowed, scores * scale, -jnp.inf)
            expo = jnp.exp(scores - jnp.max(scores, axis=1, keepdims=True))
            weights = (expo / jnp.sum(expo, axis=1, keepdims=True)).astype(jnp.bfloat16)
            mixed = jnp.dot(weights, values, preferred_element_type=jnp.float32)
            out[span, h * HEAD_DIM : (h + 1) * HEAD_DIM] = jnp.where(live, mixed, 0.0).astype(
                jnp.bfloat16
            )

    for copy in id_copies + st_copies + y_copies + c_copies + f_copies + [mid_copy] + kv_copies:
        copy.wait_send()
    for sent in z_copies:
        for copy in sent:
            copy.wait_send()


def tables(tokens):
    half = HEAD_DIM // 2
    position = np.arange(tokens, dtype=np.float32)
    inverse = np.float32(rope_base) ** (-(np.arange(half, dtype=np.float32) * 2.0) / HEAD_DIM).astype(
        np.float32
    )
    angle = position[:, None] * inverse[None, :].astype(np.float32)
    cosine = np.cos(angle)
    sine = np.sin(angle)
    return (
        np.concatenate([cosine, cosine], axis=1).astype(np.float32),
        np.concatenate([-sine, sine], axis=1).astype(np.float32),
    )


def local_fused(
    planes,
    states,
    query_weight,
    key_value_weight,
    lengths,
    adapter_ids,
    adapter_slot,
    down_store,
    query_up_store,
    key_value_store,
):
    tokens, half = states.shape
    q_cols = query_weight.shape[1]
    kv_cols = key_value_weight.shape[1]
    cols = q_cols + kv_cols
    mine, rank = query_up_store.shape[:2]
    turned = jnp.transpose(down_store, (0, 2, 1))
    rows = jnp.stack(
        [
            turned[:, :rank, :cols],
            turned[:, rank:, :cols],
            jnp.concatenate([turned[:, :rank, cols:], turned[:, rank:, cols:]], axis=2),
            jnp.concatenate([query_up_store, key_value_store], axis=2),
        ]
    )
    cosine, sine = tables(tokens)
    peers = planes - 1
    vmem = pl.BlockSpec(memory_space=pltpu.VMEM)
    smem = pl.BlockSpec(memory_space=pltpu.SMEM)
    hbm = pl.BlockSpec(memory_space=pl.ANY)
    bf16, f32 = jnp.bfloat16, jnp.float32
    dma = pltpu.SemaphoreType.DMA
    return pl.pallas_call(
        functools.partial(fused, planes),
        out_shape=jax.ShapeDtypeStruct((tokens, q_cols), bf16),
        in_specs=[smem, smem, smem, hbm, hbm, hbm, hbm, vmem, vmem],
        out_specs=vmem,
        scratch_shapes=[
            pltpu.VMEM((tokens, half), bf16),
            pltpu.VMEM((tokens, half), bf16),
            pltpu.VMEM((half, cols), bf16),
            pltpu.VMEM((half, cols), bf16),
            pltpu.VMEM((tokens, cols), f32),
            pltpu.VMEM((4, 4 * mine, rank, cols), bf16),
            pltpu.VMEM((16, 128), jnp.int32),
            pltpu.VMEM((peers, 16, 128), jnp.int32),
            pltpu.VMEM((4, peers, rank, cols), bf16),
            pltpu.VMEM((4, peers, rank, cols), bf16),
            pltpu.VMEM((2 * rank, half), bf16),
            pltpu.VMEM((4, rank, cols), bf16),
            pltpu.VMEM((2 * rank, tokens), f32),
            pltpu.VMEM((2 * rank, tokens), f32),
            pltpu.VMEM((tokens, kv_cols), bf16),
            pltpu.VMEM((tokens, HEAD_DIM), bf16),
            dma((6,)),
            dma((PIECES,)),
            dma((PIECES,)),
            dma((4,)),
            dma((4,)),
            dma((4,)),
            dma((4,)),
            dma((4,)),
            dma((4,)),
            dma((peers,)),
            dma((peers,)),
            dma((4, peers)),
            dma((4, peers)),
            dma((1,)),
            dma((1,)),
            dma((len(GROUPS),)),
            dma((len(GROUPS),)),
        ],
        compiler_params=pltpu.CompilerParams(
            collective_id=0, has_side_effects=True, vmem_limit_bytes=40 * 1024 * 1024
        ),
        name="fused_attention",
    )(adapter_ids, adapter_slot, lengths, states, query_weight, key_value_weight, rows, cosine, sine)


def solution(mesh):
    planes = mesh.shape["req"] // 4
    if mesh.shape["tp"] == 2 and planes == 4:
        body = functools.partial(local_fused, planes)
    else:
        body = local
    return jax.shard_map(
        body,
        mesh=mesh,
        in_specs=(
            P("req", "tp"),
            P(None, "tp"),
            P(None, "tp"),
            P("req"),
            P("req"),
            P(),
            P("req", "tp", None),
            P("req", None, "tp"),
            P("req", None, "tp"),
        ),
        out_specs=P("req", "tp"),
        check_vma=False,
    )
```

```python
import functools
import math

import jax
import jax.numpy as jnp
import numpy as np
from jax import lax
from jax.experimental import pallas as pl
from jax.experimental.pallas import tpu as pltpu
from jax.sharding import PartitionSpec as P

HEADS = 12
HEAD_DIM = 128


adapter_scale = 0.5
rope_base = 100000000000.0


def rotate(field):
    half = field.shape[-1] // 2
    count = field.shape[-3]
    position = jnp.arange(count).astype(jnp.float32)
    inverse = rope_base ** (-(jnp.arange(half).astype(jnp.float32) * 2.0) / field.shape[-1])
    angle = position[:, None] * inverse[None, :]
    cosine = jnp.cos(angle)[:, None, :]
    sine = jnp.sin(angle)[:, None, :]
    first_half = field[..., :half]
    second_half = field[..., half:]
    return jnp.concatenate(
        [first_half * cosine - second_half * sine, second_half * cosine + first_half * sine],
        axis=-1,
    )


def lookup_slots(wanted, adapter_slot):
    table = jnp.arange(adapter_slot.shape[0], dtype=jnp.int32)
    matches = wanted[:, None] == table[None, :]
    return jnp.sum(jnp.where(matches, adapter_slot[None, :], 0), axis=1)


def local(
    states,
    query_weight,
    key_value_weight,
    lengths,
    adapter_ids,
    adapter_slot,
    down_store,
    query_up_store,
    key_value_store,
):
    tp_index = lax.axis_index("tp")
    req_dev = lengths.shape[0]
    rows_total = states.shape[0]
    slot_len = rows_total // req_dev
    q_cols = query_weight.shape[1]
    kv_cols = key_value_weight.shape[1]
    heads_here = q_cols // HEAD_DIM
    pooled = (
        lax.all_gather(down_store, "req", axis=0, tiled=True),
        lax.all_gather(query_up_store, "req", axis=0, tiled=True),
        lax.all_gather(key_value_store, "req", axis=0, tiled=True),
    )
    own_slots = lookup_slots(adapter_ids, adapter_slot)
    adapter_down, adapter_query, adapter_pair = (
        jnp.take(member, own_slots, axis=0) for member in pooled
    )
    full_down = lax.all_gather(adapter_down, "tp", axis=1, tiled=True)
    piece = lax.all_gather(states, "tp", axis=1, tiled=True)
    width = piece.shape[1]
    grouped = piece.reshape(req_dev, slot_len, width)
    query_total = jnp.dot(piece, query_weight, preferred_element_type=jnp.float32)
    key_value_sum = jnp.dot(piece, key_value_weight, preferred_element_type=jnp.float32)
    rank_sum = jnp.einsum("rsd,rdk->rsk", grouped, full_down, preferred_element_type=jnp.float32)
    rank_mid = rank_sum.astype(jnp.bfloat16)
    rank_cols = rank_mid.shape[2] // 2
    query_addition = jnp.einsum(
        "rsk,rkc->rsc",
        rank_mid[:, :, :rank_cols],
        adapter_query,
        preferred_element_type=jnp.float32,
    ).reshape(rows_total, q_cols)
    key_value_extra = jnp.einsum(
        "rsk,rkc->rsc", rank_mid[:, :, rank_cols:], adapter_pair, preferred_element_type=jnp.float32
    ).reshape(rows_total, kv_cols)
    query_plain = query_total + adapter_scale * query_addition
    key_value_own = (key_value_sum + adapter_scale * key_value_extra).astype(jnp.bfloat16)
    pair_all = lax.all_gather(key_value_own, "tp", axis=1, tiled=True)
    key_width = pair_all.shape[1] // 2
    kv_heads = key_width // HEAD_DIM
    group = HEADS // kv_heads
    kv_index = tp_index * heads_here // group
    key_block = lax.dynamic_slice_in_dim(pair_all, kv_index * HEAD_DIM, HEAD_DIM, 1)
    value_block = lax.dynamic_slice_in_dim(pair_all, key_width + kv_index * HEAD_DIM, HEAD_DIM, 1)
    queries = rotate(query_plain.reshape(req_dev, slot_len, heads_here, HEAD_DIM)).astype(
        jnp.bfloat16
    )
    keys_one = rotate(key_block.astype(jnp.float32).reshape(req_dev, slot_len, 1, HEAD_DIM)).astype(
        jnp.bfloat16
    )[:, :, 0, :]
    values_one = value_block.reshape(req_dev, slot_len, HEAD_DIM)
    scale = 1.0 / math.sqrt(HEAD_DIM)
    scores = (
        jnp.einsum("rqhd,rkd->rhqk", queries, keys_one, preferred_element_type=jnp.float32) * scale
    )
    position = jnp.arange(slot_len, dtype=jnp.int32)
    allowed = (position[None, None, :] <= position[None, :, None]) & (
        position[None, None, :] < lengths[:, None, None]
    )
    scores = jnp.where(allowed[:, None, :, :], scores, -jnp.inf)
    highest = jnp.max(scores, axis=-1, keepdims=True)
    expo = jnp.exp(scores - highest)
    weights = (expo / jnp.sum(expo, axis=-1, keepdims=True)).astype(jnp.bfloat16)
    context = jnp.einsum("rhqk,rkd->rqhd", weights, values_one, preferred_element_type=jnp.float32)
    live_rows = position[None, :] < lengths[:, None]
    context = jnp.where(live_rows[:, :, None, None], context, 0.0)
    return context.reshape(rows_total, q_cols).astype(jnp.bfloat16)


MESH = pl.DeviceIdType.MESH
PIECES = 4
GROUPS = ((0, 192), (192, 64))


def fused(
    planes,
    ids,
    slots,
    lengths,
    states,
    wq,
    wkv,
    down_rows,
    query_rows,
    pair_rows,
    trig,
    out,
    own_st,
    other_st,
    w_own,
    w_other,
    total,
    plane_down,
    plane_up,
    cosine,
    sine,
    ids_own,
    ids_in,
    leave_down,
    leave_up,
    land_down,
    land_up,
    mid_out,
    mid_in,
    kv_own,
    kv_in,
    local_sem,
    st_send,
    st_recv,
    y_send,
    y_recv,
    c_send,
    c_recv,
    f_send,
    f_recv,
    i_send,
    i_recv,
    z_send,
    z_recv,
    m_send,
    m_recv,
    kv_send,
    kv_recv,
):
    r = lax.axis_index("req")
    tp = lax.axis_index("tp")
    per_plane = 4
    count = planes * per_plane
    half = own_st.shape[1]
    q_cols = wq.shape[1]
    tokens = own_st.shape[0]
    step = tokens // PIECES
    mine, rank, lanes = plane_down.shape[1] // per_plane, plane_up.shape[1], plane_down.shape[3]
    parts = plane_down.shape[0]
    core_peer = r + 1 - 2 * (r % 2)
    y_peer = r + 2 - 4 * ((r // 2) % 2)
    z_peers = [(r + per_plane * d) % count for d in range(1, planes)]
    across = 1 - tp
    base = (r // per_plane) * (per_plane * mine)

    def place(index):
        return pl.ds((index % per_plane) * mine, mine)

    def remote(src, dst, send, recv, who):
        return pltpu.make_async_remote_copy(
            src_ref=src, dst_ref=dst, send_sem=send, recv_sem=recv, device_id=who, device_id_type=MESH
        )

    own_rows = pl.ds(pl.multiple_of(tp * half, half), half)
    other_rows = pl.ds(pl.multiple_of(across * half, half), half)
    loads = [
        pltpu.make_async_copy(states, own_st, local_sem.at[0]),
        pltpu.make_async_copy(wq.at[own_rows], w_own.at[:, :q_cols], local_sem.at[1]),
        pltpu.make_async_copy(wkv.at[own_rows], w_own.at[:, q_cols:], local_sem.at[2]),
        pltpu.make_async_copy(wq.at[other_rows], w_other.at[:, :q_cols], local_sem.at[3]),
        pltpu.make_async_copy(wkv.at[other_rows], w_other.at[:, q_cols:], local_sem.at[4]),
        pltpu.make_async_copy(trig.at[0], cosine, local_sem.at[5]),
        pltpu.make_async_copy(trig.at[1], sine, local_sem.at[6]),
        pltpu.make_async_copy(query_rows, plane_up.at[place(r), :, :q_cols], local_sem.at[7]),
        pltpu.make_async_copy(pair_rows, plane_up.at[place(r), :, q_cols:], local_sem.at[8]),
    ] + [
        pltpu.make_async_copy(
            down_rows.at[:, :, pl.ds(k * lanes, lanes)], plane_down.at[k, place(r)], local_sem.at[9 + k]
        )
        for k in range(parts)
    ]
    for copy in loads:
        copy.start()

    ids_own[...] = jnp.full(ids_own.shape, slots[ids[0]], jnp.int32)

    barrier = pltpu.get_barrier_semaphore()
    for peer in [core_peer, y_peer] + z_peers:
        pl.semaphore_signal(barrier, inc=1, device_id={"req": peer}, device_id_type=MESH)
    pl.semaphore_signal(barrier, inc=1, device_id={"tp": across}, device_id_type=MESH)
    pl.semaphore_wait(barrier, planes + 2)

    id_copies = [
        remote(ids_own, ids_in.at[d], i_send.at[d], i_recv.at[d], {"req": peer})
        for d, peer in enumerate(z_peers)
    ]
    st_copies = [
        remote(
            states.at[pl.ds(p * step, step)],
            other_st.at[pl.ds(p * step, step)],
            st_send.at[p],
            st_recv.at[p],
            {"tp": across},
        )
        for p in range(PIECES)
    ]
    def share(peer, send, recv):
        made = [
            remote(
                down_rows.at[:, :, pl.ds(k * lanes, lanes)],
                plane_down.at[k, place(r)],
                send.at[k],
                recv.at[k],
                {"req": peer},
            )
            for k in range(parts)
        ]
        for n, (source, columns) in enumerate(
            ((query_rows, pl.ds(0, q_cols)), (pair_rows, pl.ds(q_cols, plane_up.shape[2] - q_cols)))
        ):
            made.append(
                remote(
                    source,
                    plane_up.at[place(r), :, columns],
                    send.at[parts + n],
                    recv.at[parts + n],
                    {"req": peer},
                )
            )
        return made

    y_copies = share(y_peer, y_send, y_recv)
    c_copies = share(core_peer, c_send, c_recv)
    f_copies = [
        remote(block, block, f_send.at[k], f_recv.at[k], {"req": core_peer})
        for k, block in enumerate(
            [plane_down.at[k, place(y_peer)] for k in range(parts)] + [plane_up.at[place(y_peer)]]
        )
    ]
    for copy in id_copies:
        copy.start()
    for k in range(parts + 2):
        if k < PIECES:
            st_copies[k].start()
        y_copies[k].start()
        c_copies[k].start()

    for n in (0, 1, 2):
        loads[n].wait()
    total[...] = jnp.dot(own_st[...], w_own[...], preferred_element_type=jnp.float32)
    for copy in loads[3:]:
        copy.wait()
    for copy in id_copies:
        copy.wait_recv()

    def add_piece(p):
        st_copies[p].wait_recv()
        span = pl.ds(p * step, step)
        total[span] += jnp.dot(other_st[span], w_other[...], preferred_element_type=jnp.float32)

    z_copies = []

    def stage(k):
        up = k == parts
        source = plane_up if up else plane_down.at[k]
        which = (parts, parts + 1) if up else (k,)
        for n in which:
            y_copies[n].wait_recv()
        f_copies[k].start()
        for n in which:
            c_copies[n].wait_recv()
        f_copies[k].wait_recv()

        def pick(j, sums):
            record = source[j]
            made = []
            for d in range(planes):
                wanted = ids_own[...] if d == 0 else ids_in[planes - 1 - d]
                flag = jnp.where(wanted == base + j, 1.0, 0.0).astype(jnp.bfloat16)
                flag = jnp.concatenate([flag] * (record.shape[0] // flag.shape[0]), axis=0)
                flag = jnp.concatenate([flag] * (record.shape[1] // flag.shape[1]), axis=1)
                made.append(sums[d] + flag * record)
            return tuple(made)

        zero = jnp.zeros(source.shape[1:], jnp.bfloat16)
        sums = lax.fori_loop(0, per_plane * mine, pick, (zero,) * planes)
        leave = leave_up if up else leave_down.at[k]
        land = land_up if up else land_down.at[k]
        for d in range(1, planes):
            leave[d - 1] = sums[d]
        sent = [
            remote(leave.at[d], land.at[d], z_send.at[k, d], z_recv.at[k, d], {"req": peer})
            for d, peer in enumerate(z_peers)
        ]
        for copy in sent:
            copy.start()
        z_copies.append(sent)
        return sums[0]

    def take(k, record):
        for copy in z_copies[k]:
            copy.wait_recv()
        land = land_up if k == parts else land_down.at[k]
        for d in range(planes - 1):
            record = record + land[d]
        return record

    def lower(k, record):
        part = lax.dot_general(
            take(k, record),
            own_st[:, k * lanes : (k + 1) * lanes],
            (((1,), (1,)), ((), ())),
            preferred_element_type=jnp.float32,
        )
        mid_out[...] = part if k == 0 else mid_out[...] + part

    held = None
    for k in range(parts):
        fresh = stage(k)
        if k:
            lower(k - 1, held)
        held = fresh
        if k == 1:
            add_piece(0)
    held_up = stage(parts)
    lower(parts - 1, held)
    mid_copy = remote(mid_out, mid_in, m_send.at[0], m_recv.at[0], {"tp": across})
    mid_copy.start()
    add_piece(1)
    add_piece(2)
    up = take(parts, held_up)
    mid_copy.wait_recv()
    mid = jnp.transpose(mid_out[...] + mid_in[...]).astype(jnp.bfloat16)
    total[:, q_cols:] += 0.5 * jnp.dot(
        mid[:, rank:], up[:, q_cols:], preferred_element_type=jnp.float32
    )

    kv_copies = []
    keep = pl.ds(pl.multiple_of(tp * HEAD_DIM, HEAD_DIM), HEAD_DIM)
    give = pl.ds(pl.multiple_of(across * HEAD_DIM, HEAD_DIM), HEAD_DIM)
    for g, (first, size) in enumerate(GROUPS):
        if g == 1:
            add_piece(3)
        span = pl.ds(first, size)
        kv_own[span] = total[span, q_cols:].astype(jnp.bfloat16)
        copy = remote(
            kv_own.at[span, give], kv_in.at[span], kv_send.at[g], kv_recv.at[g], {"tp": across}
        )
        copy.start()
        kv_copies.append(copy)

    total[:, :q_cols] += 0.5 * jnp.dot(
        mid[:, :rank], up[:, :q_cols], preferred_element_type=jnp.float32
    )
    scale = 1.0 / math.sqrt(HEAD_DIM)
    length = lengths[0]

    def turn(x, span):
        return (x * cosine[span] + pltpu.roll(x, HEAD_DIM // 2, 1) * sine[span]).astype(jnp.bfloat16)

    key_parts = []
    value_parts = []
    for g, (first, size) in enumerate(GROUPS):
        span = pl.ds(first, size)
        turned = [
            turn(total[span, h * HEAD_DIM : (h + 1) * HEAD_DIM], span)
            for h in range(q_cols // HEAD_DIM)
        ]
        kv_copies[g].wait_recv()
        kept = kv_own[span, keep]
        came = kv_in[span]
        first_side = jnp.full(kept.shape, tp, jnp.int32) == 0
        key = jnp.where(first_side, kept.astype(jnp.float32), came.astype(jnp.float32))
        value = jnp.where(first_side, came.astype(jnp.float32), kept.astype(jnp.float32))
        key_parts.append(turn(key, span))
        value_parts.append(value.astype(jnp.bfloat16))
        reach = first + size
        keys = jnp.concatenate(key_parts, axis=0) if g else key_parts[0]
        values = jnp.concatenate(value_parts, axis=0) if g else value_parts[0]
        row = lax.broadcasted_iota(jnp.int32, (size, reach), 0) + first
        column = lax.broadcasted_iota(jnp.int32, (size, reach), 1)
        allowed = (column <= row) & (column < length)
        live = lax.broadcasted_iota(jnp.int32, (size, HEAD_DIM), 0) + first < length
        for h, query in enumerate(turned):
            scores = lax.dot_general(
                query, keys, (((1,), (1,)), ((), ())), preferred_element_type=jnp.float32
            )
            scores = jnp.where(allowed, scores * scale, -jnp.inf)
            expo = jnp.exp(scores - jnp.max(scores, axis=1, keepdims=True))
            weights = (expo / jnp.sum(expo, axis=1, keepdims=True)).astype(jnp.bfloat16)
            mixed = jnp.dot(weights, values, preferred_element_type=jnp.float32)
            out[span, h * HEAD_DIM : (h + 1) * HEAD_DIM] = jnp.where(live, mixed, 0.0).astype(
                jnp.bfloat16
            )

    for copy in id_copies + st_copies + y_copies + c_copies + f_copies + [mid_copy] + kv_copies:
        copy.wait_send()
    for sent in z_copies:
        for copy in sent:
            copy.wait_send()


def tables(tokens):
    half = HEAD_DIM // 2
    position = np.arange(tokens, dtype=np.float32)
    inverse = np.float32(rope_base) ** (-(np.arange(half, dtype=np.float32) * 2.0) / HEAD_DIM).astype(
        np.float32
    )
    angle = position[:, None] * inverse[None, :].astype(np.float32)
    cosine = np.cos(angle)
    sine = np.sin(angle)
    return np.stack(
        [np.concatenate([cosine, cosine], axis=1), np.concatenate([-sine, sine], axis=1)]
    ).astype(np.float32)


def local_fused(
    planes,
    states,
    query_weight,
    key_value_weight,
    lengths,
    adapter_ids,
    adapter_slot,
    down_store,
    query_up_store,
    key_value_store,
):
    tokens, half = states.shape
    q_cols = query_weight.shape[1]
    kv_cols = key_value_weight.shape[1]
    cols = q_cols + kv_cols
    mine, rank = query_up_store.shape[:2]
    down_rows = jnp.transpose(down_store, (0, 2, 1))
    parts = 3
    lanes = half // parts
    trig = tables(tokens)
    peers = planes - 1
    vmem = pl.BlockSpec(memory_space=pltpu.VMEM)
    smem = pl.BlockSpec(memory_space=pltpu.SMEM)
    hbm = pl.BlockSpec(memory_space=pl.ANY)
    bf16, f32 = jnp.bfloat16, jnp.float32
    dma = pltpu.SemaphoreType.DMA
    return pl.pallas_call(
        functools.partial(fused, planes),
        out_shape=jax.ShapeDtypeStruct((tokens, q_cols), bf16),
        in_specs=[smem] * 3 + [hbm] * 7,
        out_specs=vmem,
        scratch_shapes=[
            pltpu.VMEM((tokens, half), bf16),
            pltpu.VMEM((tokens, half), bf16),
            pltpu.VMEM((half, cols), bf16),
            pltpu.VMEM((half, cols), bf16),
            pltpu.VMEM((tokens, cols), f32),
            pltpu.VMEM((parts, 4 * mine, 2 * rank, lanes), bf16),
            pltpu.VMEM((4 * mine, rank, cols), bf16),
            pltpu.VMEM((tokens, HEAD_DIM), f32),
            pltpu.VMEM((tokens, HEAD_DIM), f32),
            pltpu.VMEM((16, 128), jnp.int32),
            pltpu.VMEM((peers, 16, 128), jnp.int32),
            pltpu.VMEM((parts, peers, 2 * rank, lanes), bf16),
            pltpu.VMEM((peers, rank, cols), bf16),
            pltpu.VMEM((parts, peers, 2 * rank, lanes), bf16),
            pltpu.VMEM((peers, rank, cols), bf16),
            pltpu.VMEM((2 * rank, tokens), f32),
            pltpu.VMEM((2 * rank, tokens), f32),
            pltpu.VMEM((tokens, kv_cols), bf16),
            pltpu.VMEM((tokens, HEAD_DIM), bf16),
            dma((9 + parts,)),
            dma((PIECES,)),
            dma((PIECES,)),
            dma((parts + 2,)),
            dma((parts + 2,)),
            dma((parts + 2,)),
            dma((parts + 2,)),
            dma((parts + 1,)),
            dma((parts + 1,)),
            dma((peers,)),
            dma((peers,)),
            dma((parts + 1, peers)),
            dma((parts + 1, peers)),
            dma((1,)),
            dma((1,)),
            dma((len(GROUPS),)),
            dma((len(GROUPS),)),
        ],
        compiler_params=pltpu.CompilerParams(
            collective_id=0, has_side_effects=True, vmem_limit_bytes=60 * 1024 * 1024
        ),
        name="fused_attention",
    )(
        adapter_ids,
        adapter_slot,
        lengths,
        states,
        query_weight,
        key_value_weight,
        down_rows,
        query_up_store,
        key_value_store,
        trig,
    )


def solution(mesh):
    planes = mesh.shape["req"] // 4
    if mesh.shape["tp"] == 2 and planes == 4:
        body = functools.partial(local_fused, planes)
    else:
        body = local
    return jax.shard_map(
        body,
        mesh=mesh,
        in_specs=(
            P("req", "tp"),
            P(None, "tp"),
            P(None, "tp"),
            P("req"),
            P("req"),
            P(),
            P("req", "tp", None),
            P("req", None, "tp"),
            P("req", None, "tp"),
        ),
        out_specs=P("req", "tp"),
        check_vma=False,
    )
```

```python
import functools
import math

import jax
import jax.numpy as jnp
import numpy as np
from jax import lax
from jax.experimental import pallas as pl
from jax.experimental.pallas import tpu as pltpu
from jax.sharding import PartitionSpec as P

HEADS = 12
HEAD_DIM = 128


adapter_scale = 0.5
rope_base = 100000000000.0


def rotate(field):
    half = field.shape[-1] // 2
    count = field.shape[-3]
    position = jnp.arange(count).astype(jnp.float32)
    inverse = rope_base ** (-(jnp.arange(half).astype(jnp.float32) * 2.0) / field.shape[-1])
    angle = position[:, None] * inverse[None, :]
    cosine = jnp.cos(angle)[:, None, :]
    sine = jnp.sin(angle)[:, None, :]
    first_half = field[..., :half]
    second_half = field[..., half:]
    return jnp.concatenate(
        [first_half * cosine - second_half * sine, second_half * cosine + first_half * sine],
        axis=-1,
    )


def lookup_slots(wanted, adapter_slot):
    table = jnp.arange(adapter_slot.shape[0], dtype=jnp.int32)
    matches = wanted[:, None] == table[None, :]
    return jnp.sum(jnp.where(matches, adapter_slot[None, :], 0), axis=1)


def local(
    states,
    query_weight,
    key_value_weight,
    lengths,
    adapter_ids,
    adapter_slot,
    down_store,
    query_up_store,
    key_value_store,
):
    tp_index = lax.axis_index("tp")
    req_dev = lengths.shape[0]
    rows_total = states.shape[0]
    slot_len = rows_total // req_dev
    q_cols = query_weight.shape[1]
    kv_cols = key_value_weight.shape[1]
    heads_here = q_cols // HEAD_DIM
    pooled = (
        lax.all_gather(down_store, "req", axis=0, tiled=True),
        lax.all_gather(query_up_store, "req", axis=0, tiled=True),
        lax.all_gather(key_value_store, "req", axis=0, tiled=True),
    )
    own_slots = lookup_slots(adapter_ids, adapter_slot)
    adapter_down, adapter_query, adapter_pair = (
        jnp.take(member, own_slots, axis=0) for member in pooled
    )
    full_down = lax.all_gather(adapter_down, "tp", axis=1, tiled=True)
    piece = lax.all_gather(states, "tp", axis=1, tiled=True)
    width = piece.shape[1]
    grouped = piece.reshape(req_dev, slot_len, width)
    query_total = jnp.dot(piece, query_weight, preferred_element_type=jnp.float32)
    key_value_sum = jnp.dot(piece, key_value_weight, preferred_element_type=jnp.float32)
    rank_sum = jnp.einsum("rsd,rdk->rsk", grouped, full_down, preferred_element_type=jnp.float32)
    rank_mid = rank_sum.astype(jnp.bfloat16)
    rank_cols = rank_mid.shape[2] // 2
    query_addition = jnp.einsum(
        "rsk,rkc->rsc",
        rank_mid[:, :, :rank_cols],
        adapter_query,
        preferred_element_type=jnp.float32,
    ).reshape(rows_total, q_cols)
    key_value_extra = jnp.einsum(
        "rsk,rkc->rsc", rank_mid[:, :, rank_cols:], adapter_pair, preferred_element_type=jnp.float32
    ).reshape(rows_total, kv_cols)
    query_plain = query_total + adapter_scale * query_addition
    key_value_own = (key_value_sum + adapter_scale * key_value_extra).astype(jnp.bfloat16)
    pair_all = lax.all_gather(key_value_own, "tp", axis=1, tiled=True)
    key_width = pair_all.shape[1] // 2
    kv_heads = key_width // HEAD_DIM
    group = HEADS // kv_heads
    kv_index = tp_index * heads_here // group
    key_block = lax.dynamic_slice_in_dim(pair_all, kv_index * HEAD_DIM, HEAD_DIM, 1)
    value_block = lax.dynamic_slice_in_dim(pair_all, key_width + kv_index * HEAD_DIM, HEAD_DIM, 1)
    queries = rotate(query_plain.reshape(req_dev, slot_len, heads_here, HEAD_DIM)).astype(
        jnp.bfloat16
    )
    keys_one = rotate(key_block.astype(jnp.float32).reshape(req_dev, slot_len, 1, HEAD_DIM)).astype(
        jnp.bfloat16
    )[:, :, 0, :]
    values_one = value_block.reshape(req_dev, slot_len, HEAD_DIM)
    scale = 1.0 / math.sqrt(HEAD_DIM)
    scores = (
        jnp.einsum("rqhd,rkd->rhqk", queries, keys_one, preferred_element_type=jnp.float32) * scale
    )
    position = jnp.arange(slot_len, dtype=jnp.int32)
    allowed = (position[None, None, :] <= position[None, :, None]) & (
        position[None, None, :] < lengths[:, None, None]
    )
    scores = jnp.where(allowed[:, None, :, :], scores, -jnp.inf)
    highest = jnp.max(scores, axis=-1, keepdims=True)
    expo = jnp.exp(scores - highest)
    weights = (expo / jnp.sum(expo, axis=-1, keepdims=True)).astype(jnp.bfloat16)
    context = jnp.einsum("rhqk,rkd->rqhd", weights, values_one, preferred_element_type=jnp.float32)
    live_rows = position[None, :] < lengths[:, None]
    context = jnp.where(live_rows[:, :, None, None], context, 0.0)
    return context.reshape(rows_total, q_cols).astype(jnp.bfloat16)


MESH = pl.DeviceIdType.MESH
PIECES = 4
GROUPS = ((0, 192), (192, 64))


def fused(
    planes,
    ids,
    slots,
    lengths,
    states,
    wq,
    wkv,
    down_rows,
    query_rows,
    pair_rows,
    trig,
    out,
    own_st,
    other_st,
    w_own,
    w_other,
    total,
    plane_down,
    plane_up,
    cosine,
    sine,
    ids_own,
    ids_in,
    leave_down,
    leave_up,
    land_down,
    land_up,
    mid_out,
    mid_in,
    kv_own,
    kv_in,
    local_sem,
    st_send,
    st_recv,
    y_send,
    y_recv,
    c_send,
    c_recv,
    f_send,
    f_recv,
    i_send,
    i_recv,
    z_send,
    z_recv,
    m_send,
    m_recv,
    kv_send,
    kv_recv,
):
    r = lax.axis_index("req")
    tp = lax.axis_index("tp")
    per_plane = 4
    count = planes * per_plane
    half = own_st.shape[1]
    q_cols = wq.shape[1]
    tokens = own_st.shape[0]
    step = tokens // PIECES
    mine, rank, lanes = plane_down.shape[1] // per_plane, plane_up.shape[1], plane_down.shape[3]
    parts = plane_down.shape[0]
    core_peer = r + 1 - 2 * (r % 2)
    y_peer = r + 2 - 4 * ((r // 2) % 2)
    z_peers = [(r + per_plane * d) % count for d in range(1, planes)]
    across = 1 - tp
    base = (r // per_plane) * (per_plane * mine)

    def place(index):
        return pl.ds((index % per_plane) * mine, mine)

    def remote(src, dst, send, recv, who):
        return pltpu.make_async_remote_copy(
            src_ref=src, dst_ref=dst, send_sem=send, recv_sem=recv, device_id=who, device_id_type=MESH
        )

    own_rows = pl.ds(pl.multiple_of(tp * half, half), half)
    other_rows = pl.ds(pl.multiple_of(across * half, half), half)
    loads = [
        pltpu.make_async_copy(states, own_st, local_sem.at[0]),
        pltpu.make_async_copy(wq.at[own_rows], w_own.at[:, :q_cols], local_sem.at[1]),
        pltpu.make_async_copy(wkv.at[own_rows], w_own.at[:, q_cols:], local_sem.at[2]),
        pltpu.make_async_copy(wq.at[other_rows], w_other.at[:, :q_cols], local_sem.at[3]),
        pltpu.make_async_copy(wkv.at[other_rows], w_other.at[:, q_cols:], local_sem.at[4]),
        pltpu.make_async_copy(trig.at[0], cosine, local_sem.at[5]),
        pltpu.make_async_copy(trig.at[1], sine, local_sem.at[6]),
        pltpu.make_async_copy(query_rows, plane_up.at[place(r), :, :q_cols], local_sem.at[7]),
        pltpu.make_async_copy(pair_rows, plane_up.at[place(r), :, q_cols:], local_sem.at[8]),
    ] + [
        pltpu.make_async_copy(
            down_rows.at[:, :, pl.ds(k * lanes, lanes)], plane_down.at[k, place(r)], local_sem.at[9 + k]
        )
        for k in range(parts)
    ]
    for copy in loads:
        copy.start()

    ids_own[...] = jnp.full(ids_own.shape, slots[ids[0]], jnp.int32)

    barrier = pltpu.get_barrier_semaphore()
    for peer in [core_peer, y_peer] + z_peers:
        pl.semaphore_signal(barrier, inc=1, device_id={"req": peer}, device_id_type=MESH)
    pl.semaphore_signal(barrier, inc=1, device_id={"tp": across}, device_id_type=MESH)
    pl.semaphore_wait(barrier, planes + 2)

    id_copies = [
        remote(ids_own, ids_in.at[d], i_send.at[d], i_recv.at[d], {"req": peer})
        for d, peer in enumerate(z_peers)
    ]
    st_copies = [
        remote(
            states.at[pl.ds(p * step, step)],
            other_st.at[pl.ds(p * step, step)],
            st_send.at[p],
            st_recv.at[p],
            {"tp": across},
        )
        for p in range(PIECES)
    ]
    def share(peer, send, recv):
        made = [
            remote(
                down_rows.at[:, :, pl.ds(k * lanes, lanes)],
                plane_down.at[k, place(r)],
                send.at[k],
                recv.at[k],
                {"req": peer},
            )
            for k in range(parts)
        ]
        for n, (source, columns) in enumerate(
            ((query_rows, pl.ds(0, q_cols)), (pair_rows, pl.ds(q_cols, plane_up.shape[2] - q_cols)))
        ):
            made.append(
                remote(
                    source,
                    plane_up.at[place(r), :, columns],
                    send.at[parts + n],
                    recv.at[parts + n],
                    {"req": peer},
                )
            )
        return made

    y_copies = share(y_peer, y_send, y_recv)
    c_copies = share(core_peer, c_send, c_recv)
    f_copies = [
        remote(block, block, f_send.at[k], f_recv.at[k], {"req": core_peer})
        for k, block in enumerate(
            [plane_down.at[k, place(y_peer)] for k in range(parts)] + [plane_up.at[place(y_peer)]]
        )
    ]
    for copy in id_copies:
        copy.start()
    for k in range(parts + 2):
        if k < PIECES - 1:
            st_copies[k].start()
        y_copies[k].start()
        c_copies[k].start()

    for n in (0, 1, 2):
        loads[n].wait()
    total[...] = jnp.dot(own_st[...], w_own[...], preferred_element_type=jnp.float32)
    for copy in loads[3:]:
        copy.wait()
    for copy in id_copies:
        copy.wait_recv()

    def add_piece(p, columns=slice(None)):
        span = pl.ds(p * step, step)
        total[span, columns] += jnp.dot(
            other_st[span], w_other[:, columns], preferred_element_type=jnp.float32
        )

    z_copies = []

    def stage(k):
        up = k == parts
        source = plane_up if up else plane_down.at[k]
        which = (parts, parts + 1) if up else (k,)
        for n in which:
            y_copies[n].wait_recv()
        f_copies[k].start()
        for n in which:
            c_copies[n].wait_recv()
        f_copies[k].wait_recv()

        def pick(j, sums):
            record = source[j]
            made = []
            for d in range(planes):
                wanted = ids_own[...] if d == 0 else ids_in[planes - 1 - d]
                flag = jnp.where(wanted == base + j, 1.0, 0.0).astype(jnp.bfloat16)
                flag = jnp.concatenate([flag] * (record.shape[0] // flag.shape[0]), axis=0)
                flag = jnp.concatenate([flag] * (record.shape[1] // flag.shape[1]), axis=1)
                made.append(sums[d] + flag * record)
            return tuple(made)

        zero = jnp.zeros(source.shape[1:], jnp.bfloat16)
        sums = lax.fori_loop(0, per_plane * mine, pick, (zero,) * planes)
        leave = leave_up if up else leave_down.at[k]
        land = land_up if up else land_down.at[k]
        for d in range(1, planes):
            leave[d - 1] = sums[d]
        sent = [
            remote(leave.at[d], land.at[d], z_send.at[k, d], z_recv.at[k, d], {"req": peer})
            for d, peer in enumerate(z_peers)
        ]
        for copy in sent:
            copy.start()
        z_copies.append(sent)
        return sums[0]

    def take(k, record):
        for copy in z_copies[k]:
            copy.wait_recv()
        land = land_up if k == parts else land_down.at[k]
        for d in range(planes - 1):
            record = record + land[d]
        return record

    def lower(k, record):
        part = lax.dot_general(
            take(k, record),
            own_st[:, k * lanes : (k + 1) * lanes],
            (((1,), (1,)), ((), ())),
            preferred_element_type=jnp.float32,
        )
        mid_out[...] = part if k == 0 else mid_out[...] + part

    held = None
    for k in range(parts):
        fresh = stage(k)
        if k:
            lower(k - 1, held)
        held = fresh
        if k in (2, 5):
            st_copies[k // 3].wait_recv()
            add_piece(k // 3)
    held_up = stage(parts)
    lower(parts - 1, held)
    mid_copy = remote(mid_out, mid_in, m_send.at[0], m_recv.at[0], {"tp": across})
    mid_copy.start()
    st_copies[PIECES - 1].start()
    st_copies[2].wait_recv()
    add_piece(2)
    up = take(parts, held_up)
    mid_copy.wait_recv()
    mid = jnp.transpose(mid_out[...] + mid_in[...]).astype(jnp.bfloat16)
    total[:, q_cols:] += 0.5 * jnp.dot(
        mid[:, rank:], up[:, q_cols:], preferred_element_type=jnp.float32
    )

    keep = pl.ds(pl.multiple_of(tp * HEAD_DIM, HEAD_DIM), HEAD_DIM)
    give = pl.ds(pl.multiple_of(across * HEAD_DIM, HEAD_DIM), HEAD_DIM)
    scale = 1.0 / math.sqrt(HEAD_DIM)
    length = lengths[0]
    kv_copies = []
    key_parts = []
    value_parts = []

    def turn(x, span):
        return (x * cosine[span] + pltpu.roll(x, HEAD_DIM // 2, 1) * sine[span]).astype(jnp.bfloat16)

    def swap(g):
        span = pl.ds(*GROUPS[g])
        kv_own[span] = total[span, q_cols:].astype(jnp.bfloat16)
        copy = remote(
            kv_own.at[span, give], kv_in.at[span], kv_send.at[g], kv_recv.at[g], {"tp": across}
        )
        copy.start()
        kv_copies.append(copy)

    def attend(g):
        first, size = GROUPS[g]
        span = pl.ds(first, size)
        turned = [
            turn(total[span, h * HEAD_DIM : (h + 1) * HEAD_DIM], span)
            for h in range(q_cols // HEAD_DIM)
        ]
        reach = first + size
        row = lax.broadcasted_iota(jnp.int32, (size, reach), 0) + first
        column = lax.broadcasted_iota(jnp.int32, (size, reach), 1)
        allowed = (column <= row) & (column < length)
        kv_copies[g].wait_recv()
        kept = kv_own[span, keep]
        came = kv_in[span]
        first_side = jnp.full(kept.shape, tp, jnp.int32) == 0
        key = jnp.where(first_side, kept.astype(jnp.float32), came.astype(jnp.float32))
        value = jnp.where(first_side, came.astype(jnp.float32), kept.astype(jnp.float32))
        key_parts.append(turn(key, span))
        value_parts.append(value.astype(jnp.bfloat16))
        keys = jnp.concatenate(key_parts, axis=0)
        values = jnp.concatenate(value_parts, axis=0)
        for h, query in enumerate(turned):
            scores = lax.dot_general(
                query, keys, (((1,), (1,)), ((), ())), preferred_element_type=jnp.float32
            )
            scores = jnp.where(allowed, scores * scale, -jnp.inf)
            expo = jnp.exp(scores - jnp.max(scores, axis=1, keepdims=True))
            share_of = 1.0 / jnp.sum(expo, axis=1, keepdims=True)
            weights = (expo * share_of).astype(jnp.bfloat16)
            mixed = jnp.dot(weights, values, preferred_element_type=jnp.float32)
            out[span, h * HEAD_DIM : (h + 1) * HEAD_DIM] = mixed.astype(jnp.bfloat16)

    swap(0)
    total[:, :q_cols] += 0.5 * jnp.dot(
        mid[:, :rank], up[:, :q_cols], preferred_element_type=jnp.float32
    )
    attend(0)
    st_copies[PIECES - 1].wait_recv()
    add_piece(PIECES - 1, slice(q_cols, None))
    swap(1)
    add_piece(PIECES - 1, slice(0, q_cols))
    attend(1)

    for copy in id_copies + st_copies + y_copies + c_copies + f_copies + [mid_copy] + kv_copies:
        copy.wait_send()
    for sent in z_copies:
        for copy in sent:
            copy.wait_send()


def tables(tokens):
    half = HEAD_DIM // 2
    position = np.arange(tokens, dtype=np.float32)
    inverse = np.float32(rope_base) ** (-(np.arange(half, dtype=np.float32) * 2.0) / HEAD_DIM).astype(
        np.float32
    )
    angle = position[:, None] * inverse[None, :].astype(np.float32)
    cosine = np.cos(angle)
    sine = np.sin(angle)
    return np.stack(
        [np.concatenate([cosine, cosine], axis=1), np.concatenate([-sine, sine], axis=1)]
    ).astype(np.float32)


def local_fused(
    planes,
    states,
    query_weight,
    key_value_weight,
    lengths,
    adapter_ids,
    adapter_slot,
    down_store,
    query_up_store,
    key_value_store,
):
    tokens, half = states.shape
    q_cols = query_weight.shape[1]
    kv_cols = key_value_weight.shape[1]
    cols = q_cols + kv_cols
    mine, rank = query_up_store.shape[:2]
    down_rows = jnp.transpose(down_store, (0, 2, 1))
    parts = 6
    lanes = half // parts
    trig = tables(tokens)
    peers = planes - 1
    vmem = pl.BlockSpec(memory_space=pltpu.VMEM)
    smem = pl.BlockSpec(memory_space=pltpu.SMEM)
    hbm = pl.BlockSpec(memory_space=pl.ANY)
    bf16, f32 = jnp.bfloat16, jnp.float32
    dma = pltpu.SemaphoreType.DMA
    context = pl.pallas_call(
        functools.partial(fused, planes),
        out_shape=jax.ShapeDtypeStruct((tokens, q_cols), bf16),
        in_specs=[smem] * 3 + [hbm] * 7,
        out_specs=vmem,
        scratch_shapes=[
            pltpu.VMEM((tokens, half), bf16),
            pltpu.VMEM((tokens, half), bf16),
            pltpu.VMEM((half, cols), bf16),
            pltpu.VMEM((half, cols), bf16),
            pltpu.VMEM((tokens, cols), f32),
            pltpu.VMEM((parts, 4 * mine, 2 * rank, lanes), bf16),
            pltpu.VMEM((4 * mine, rank, cols), bf16),
            pltpu.VMEM((tokens, HEAD_DIM), f32),
            pltpu.VMEM((tokens, HEAD_DIM), f32),
            pltpu.VMEM((16, 128), jnp.int32),
            pltpu.VMEM((peers, 16, 128), jnp.int32),
            pltpu.VMEM((parts, peers, 2 * rank, lanes), bf16),
            pltpu.VMEM((peers, rank, cols), bf16),
            pltpu.VMEM((parts, peers, 2 * rank, lanes), bf16),
            pltpu.VMEM((peers, rank, cols), bf16),
            pltpu.VMEM((2 * rank, tokens), f32),
            pltpu.VMEM((2 * rank, tokens), f32),
            pltpu.VMEM((tokens, kv_cols), bf16),
            pltpu.VMEM((tokens, HEAD_DIM), bf16),
            dma((9 + parts,)),
            dma((PIECES,)),
            dma((PIECES,)),
            dma((parts + 2,)),
            dma((parts + 2,)),
            dma((parts + 2,)),
            dma((parts + 2,)),
            dma((parts + 1,)),
            dma((parts + 1,)),
            dma((peers,)),
            dma((peers,)),
            dma((parts + 1, peers)),
            dma((parts + 1, peers)),
            dma((1,)),
            dma((1,)),
            dma((len(GROUPS),)),
            dma((len(GROUPS),)),
        ],
        compiler_params=pltpu.CompilerParams(
            collective_id=0, has_side_effects=True, vmem_limit_bytes=60 * 1024 * 1024
        ),
        name="fused_attention",
    )(
        adapter_ids,
        adapter_slot,
        lengths,
        states,
        query_weight,
        key_value_weight,
        down_rows,
        query_up_store,
        key_value_store,
        trig,
    )
    live = lax.broadcasted_iota(jnp.int32, context.shape, 0) < lengths[0]
    return jnp.where(live, context, jnp.zeros_like(context))


def solution(mesh):
    planes = mesh.shape["req"] // 4
    if mesh.shape["tp"] == 2 and planes == 4:
        body = functools.partial(local_fused, planes)
    else:
        body = local
    return jax.shard_map(
        body,
        mesh=mesh,
        in_specs=(
            P("req", "tp"),
            P(None, "tp"),
            P(None, "tp"),
            P("req"),
            P("req"),
            P(),
            P("req", "tp", None),
            P("req", None, "tp"),
            P("req", None, "tp"),
        ),
        out_specs=P("req", "tp"),
        check_vma=False,
    )
```

```python
import functools
import math

import jax
import jax.numpy as jnp
import numpy as np
from jax import lax
from jax.experimental import pallas as pl
from jax.experimental.pallas import tpu as pltpu
from jax.sharding import PartitionSpec as P

HEADS = 12
HEAD_DIM = 128


adapter_scale = 0.5
rope_base = 100000000000.0


def rotate(field):
    half = field.shape[-1] // 2
    count = field.shape[-3]
    position = jnp.arange(count).astype(jnp.float32)
    inverse = rope_base ** (-(jnp.arange(half).astype(jnp.float32) * 2.0) / field.shape[-1])
    angle = position[:, None] * inverse[None, :]
    cosine = jnp.cos(angle)[:, None, :]
    sine = jnp.sin(angle)[:, None, :]
    first_half = field[..., :half]
    second_half = field[..., half:]
    return jnp.concatenate(
        [first_half * cosine - second_half * sine, second_half * cosine + first_half * sine],
        axis=-1,
    )


def lookup_slots(wanted, adapter_slot):
    table = jnp.arange(adapter_slot.shape[0], dtype=jnp.int32)
    matches = wanted[:, None] == table[None, :]
    return jnp.sum(jnp.where(matches, adapter_slot[None, :], 0), axis=1)


def local(
    states,
    query_weight,
    key_value_weight,
    lengths,
    adapter_ids,
    adapter_slot,
    down_store,
    query_up_store,
    key_value_store,
):
    tp_index = lax.axis_index("tp")
    req_dev = lengths.shape[0]
    rows_total = states.shape[0]
    slot_len = rows_total // req_dev
    q_cols = query_weight.shape[1]
    kv_cols = key_value_weight.shape[1]
    heads_here = q_cols // HEAD_DIM
    pooled = (
        lax.all_gather(down_store, "req", axis=0, tiled=True),
        lax.all_gather(query_up_store, "req", axis=0, tiled=True),
        lax.all_gather(key_value_store, "req", axis=0, tiled=True),
    )
    own_slots = lookup_slots(adapter_ids, adapter_slot)
    adapter_down, adapter_query, adapter_pair = (
        jnp.take(member, own_slots, axis=0) for member in pooled
    )
    full_down = lax.all_gather(adapter_down, "tp", axis=1, tiled=True)
    piece = lax.all_gather(states, "tp", axis=1, tiled=True)
    width = piece.shape[1]
    grouped = piece.reshape(req_dev, slot_len, width)
    query_total = jnp.dot(piece, query_weight, preferred_element_type=jnp.float32)
    key_value_sum = jnp.dot(piece, key_value_weight, preferred_element_type=jnp.float32)
    rank_sum = jnp.einsum("rsd,rdk->rsk", grouped, full_down, preferred_element_type=jnp.float32)
    rank_mid = rank_sum.astype(jnp.bfloat16)
    rank_cols = rank_mid.shape[2] // 2
    query_addition = jnp.einsum(
        "rsk,rkc->rsc",
        rank_mid[:, :, :rank_cols],
        adapter_query,
        preferred_element_type=jnp.float32,
    ).reshape(rows_total, q_cols)
    key_value_extra = jnp.einsum(
        "rsk,rkc->rsc", rank_mid[:, :, rank_cols:], adapter_pair, preferred_element_type=jnp.float32
    ).reshape(rows_total, kv_cols)
    query_plain = query_total + adapter_scale * query_addition
    key_value_own = (key_value_sum + adapter_scale * key_value_extra).astype(jnp.bfloat16)
    pair_all = lax.all_gather(key_value_own, "tp", axis=1, tiled=True)
    key_width = pair_all.shape[1] // 2
    kv_heads = key_width // HEAD_DIM
    group = HEADS // kv_heads
    kv_index = tp_index * heads_here // group
    key_block = lax.dynamic_slice_in_dim(pair_all, kv_index * HEAD_DIM, HEAD_DIM, 1)
    value_block = lax.dynamic_slice_in_dim(pair_all, key_width + kv_index * HEAD_DIM, HEAD_DIM, 1)
    queries = rotate(query_plain.reshape(req_dev, slot_len, heads_here, HEAD_DIM)).astype(
        jnp.bfloat16
    )
    keys_one = rotate(key_block.astype(jnp.float32).reshape(req_dev, slot_len, 1, HEAD_DIM)).astype(
        jnp.bfloat16
    )[:, :, 0, :]
    values_one = value_block.reshape(req_dev, slot_len, HEAD_DIM)
    scale = 1.0 / math.sqrt(HEAD_DIM)
    scores = (
        jnp.einsum("rqhd,rkd->rhqk", queries, keys_one, preferred_element_type=jnp.float32) * scale
    )
    position = jnp.arange(slot_len, dtype=jnp.int32)
    allowed = (position[None, None, :] <= position[None, :, None]) & (
        position[None, None, :] < lengths[:, None, None]
    )
    scores = jnp.where(allowed[:, None, :, :], scores, -jnp.inf)
    highest = jnp.max(scores, axis=-1, keepdims=True)
    expo = jnp.exp(scores - highest)
    weights = (expo / jnp.sum(expo, axis=-1, keepdims=True)).astype(jnp.bfloat16)
    context = jnp.einsum("rhqk,rkd->rqhd", weights, values_one, preferred_element_type=jnp.float32)
    live_rows = position[None, :] < lengths[:, None]
    context = jnp.where(live_rows[:, :, None, None], context, 0.0)
    return context.reshape(rows_total, q_cols).astype(jnp.bfloat16)


MESH = pl.DeviceIdType.MESH
PIECES = 4
GROUPS = ((0, 192), (192, 64))


def fused(
    planes,
    ids,
    slots,
    lengths,
    states,
    wq,
    wkv,
    down_rows,
    query_rows,
    pair_rows,
    trig,
    out,
    own_st,
    other_st,
    w_own,
    w_other,
    total,
    plane_down,
    plane_up,
    cosine,
    sine,
    ids_own,
    ids_in,
    flags,
    leave_down,
    leave_up,
    land_down,
    land_up,
    mid_out,
    mid_in,
    kv_own,
    kv_in,
    local_sem,
    st_send,
    st_recv,
    y_send,
    y_recv,
    c_send,
    c_recv,
    f_send,
    f_recv,
    i_send,
    i_recv,
    z_send,
    z_recv,
    m_send,
    m_recv,
    kv_send,
    kv_recv,
):
    r = lax.axis_index("req")
    tp = lax.axis_index("tp")
    per_plane = 4
    count = planes * per_plane
    half = own_st.shape[1]
    q_cols = wq.shape[1]
    tokens = own_st.shape[0]
    step = tokens // PIECES
    mine, rank, lanes = plane_up.shape[0] // per_plane, plane_up.shape[1], land_down.shape[3]
    parts = land_down.shape[0]
    core_peer = r + 1 - 2 * (r % 2)
    y_peer = r + 2 - 4 * ((r // 2) % 2)
    z_peers = [(r + per_plane * d) % count for d in range(1, planes)]
    across = 1 - tp
    base = (r // per_plane) * (per_plane * mine)

    def place(index):
        return pl.ds((index % per_plane) * mine, mine)

    def remote(src, dst, send, recv, who):
        return pltpu.make_async_remote_copy(
            src_ref=src, dst_ref=dst, send_sem=send, recv_sem=recv, device_id=who, device_id_type=MESH
        )

    own_rows = pl.ds(pl.multiple_of(tp * half, half), half)
    other_rows = pl.ds(pl.multiple_of(across * half, half), half)
    loads = [
        pltpu.make_async_copy(states, own_st, local_sem.at[0]),
        pltpu.make_async_copy(wq.at[own_rows], w_own.at[:, :q_cols], local_sem.at[1]),
        pltpu.make_async_copy(wkv.at[own_rows], w_own.at[:, q_cols:], local_sem.at[2]),
        pltpu.make_async_copy(wq.at[other_rows], w_other.at[:, :q_cols], local_sem.at[3]),
        pltpu.make_async_copy(wkv.at[other_rows], w_other.at[:, q_cols:], local_sem.at[4]),
        pltpu.make_async_copy(trig.at[0], cosine, local_sem.at[5]),
        pltpu.make_async_copy(trig.at[1], sine, local_sem.at[6]),
        pltpu.make_async_copy(query_rows, plane_up.at[place(r), :, :q_cols], local_sem.at[7]),
        pltpu.make_async_copy(pair_rows, plane_up.at[place(r), :, q_cols:], local_sem.at[8]),
        pltpu.make_async_copy(down_rows, plane_down.at[place(r)], local_sem.at[9]),
    ]
    for copy in loads:
        copy.start()

    ids_own[...] = jnp.full(ids_own.shape, slots[ids[0]], jnp.int32)

    barrier = pltpu.get_barrier_semaphore()
    for peer in [core_peer, y_peer] + z_peers:
        pl.semaphore_signal(barrier, inc=1, device_id={"req": peer}, device_id_type=MESH)
    pl.semaphore_signal(barrier, inc=1, device_id={"tp": across}, device_id_type=MESH)
    pl.semaphore_wait(barrier, planes + 2)

    id_copies = [
        remote(ids_own, ids_in.at[d], i_send.at[d], i_recv.at[d], {"req": peer})
        for d, peer in enumerate(z_peers)
    ]
    st_copies = [
        remote(
            states.at[pl.ds(p * step, step)],
            other_st.at[pl.ds(p * step, step)],
            st_send.at[p],
            st_recv.at[p],
            {"tp": across},
        )
        for p in range(PIECES)
    ]
    def share(peer, send, recv, cuts):
        wide = half // cuts
        made = [
            remote(
                down_rows.at[:, :, pl.ds(k * wide, wide)],
                plane_down.at[place(r), :, pl.ds(k * wide, wide)],
                send.at[k],
                recv.at[k],
                {"req": peer},
            )
            for k in range(cuts)
        ]
        for n, (source, columns) in enumerate(
            ((query_rows, pl.ds(0, q_cols)), (pair_rows, pl.ds(q_cols, plane_up.shape[2] - q_cols)))
        ):
            made.append(
                remote(
                    source,
                    plane_up.at[place(r), :, columns],
                    send.at[cuts + n],
                    recv.at[cuts + n],
                    {"req": peer},
                )
            )
        return made

    y_copies = share(y_peer, y_send, y_recv, parts)
    c_copies = share(core_peer, c_send, c_recv, 1)
    f_copies = [
        remote(block, block, f_send.at[k], f_recv.at[k], {"req": core_peer})
        for k, block in enumerate(
            [plane_down.at[place(y_peer), :, pl.ds(k * lanes, lanes)] for k in range(parts)]
            + [plane_up.at[place(y_peer)]]
        )
    ]
    y_copies[0].start()
    st_copies[0].start()
    for copy in id_copies + y_copies[1:] + c_copies + st_copies[1:]:
        copy.start()

    for n in (0, 1, 2):
        loads[n].wait()
    total[...] = jnp.dot(own_st[...], w_own[...], preferred_element_type=jnp.float32)
    for copy in loads[3:]:
        copy.wait()
    for copy in id_copies:
        copy.wait_recv()

    def add_piece(p, columns=slice(None)):
        span = pl.ds(p * step, step)
        total[span, columns] += jnp.dot(
            other_st[span], w_other[:, columns], preferred_element_type=jnp.float32
        )

    z_copies = []

    for d in range(planes):
        wanted = ids_own[...] if d == 0 else ids_in[planes - 1 - d]
        for j in range(per_plane * mine):
            flags[d, j] = jnp.where(wanted == base + j, 1.0, 0.0).astype(jnp.bfloat16)

    def forward(k):
        for n in (parts, parts + 1) if k == parts else (k,):
            y_copies[n].wait_recv()
        f_copies[k].start()

    def stage(k):
        up = k == parts
        if up or k == 0:
            for copy in c_copies[1:] if up else c_copies[:1]:
                copy.wait_recv()
        f_copies[k].wait_recv()
        kept = []
        leave = leave_up if up else leave_down.at[k]
        land = land_up if up else land_down.at[k]
        for top in range(0, land.shape[1], 16):
            sums = [None] * planes
            for j in range(per_plane * mine):
                if up:
                    record = plane_up[j, top : top + 16]
                else:
                    record = plane_down[j, top : top + 16, k * lanes : (k + 1) * lanes]
                for d in range(planes):
                    flag = flags[d, j]
                    flag = jnp.concatenate([flag] * (record.shape[1] // flag.shape[1]), axis=1)
                    sums[d] = flag * record if j == 0 else sums[d] + flag * record
            for d in range(1, planes):
                leave[d - 1, top : top + 16] = sums[d]
            kept.append(sums[0])
        sent = [
            remote(leave.at[d], land.at[d], z_send.at[k, d], z_recv.at[k, d], {"req": peer})
            for d, peer in enumerate(z_peers)
        ]
        for copy in sent:
            copy.start()
        z_copies.append(sent)
        return jnp.concatenate(kept, axis=0)

    def take(k, record):
        for copy in z_copies[k]:
            copy.wait_recv()
        land = land_up if k == parts else land_down.at[k]
        for d in range(planes - 1):
            record = record + land[d]
        return record

    def lower(k, record):
        part = lax.dot_general(
            take(k, record),
            own_st[:, k * lanes : (k + 1) * lanes],
            (((1,), (1,)), ((), ())),
            preferred_element_type=jnp.float32,
        )
        mid_out[...] = part if k == 0 else mid_out[...] + part

    held = []
    forward(0)
    forward(1)
    held.append(stage(0))
    forward(2)
    held.append(stage(1))
    lower(0, held[0])
    held.append(stage(2))
    st_copies[0].wait_recv()
    add_piece(0)
    lower(1, held[1])
    forward(parts)
    held_up = stage(parts)
    lower(2, held[2])
    mid_copy = remote(mid_out, mid_in, m_send.at[0], m_recv.at[0], {"tp": across})
    mid_copy.start()
    for p in (1, 2):
        st_copies[p].wait_recv()
        add_piece(p)
    up = take(parts, held_up)
    mid_copy.wait_recv()
    mid = jnp.transpose(mid_out[...] + mid_in[...]).astype(jnp.bfloat16)
    total[:, q_cols:] += 0.5 * jnp.dot(
        mid[:, rank:], up[:, q_cols:], preferred_element_type=jnp.float32
    )

    keep = pl.ds(pl.multiple_of(tp * HEAD_DIM, HEAD_DIM), HEAD_DIM)
    give = pl.ds(pl.multiple_of(across * HEAD_DIM, HEAD_DIM), HEAD_DIM)
    scale = 1.0 / math.sqrt(HEAD_DIM)
    length = lengths[0]
    kv_copies = []
    key_parts = []
    value_parts = []

    def turn(x, span):
        return (x * cosine[span] + pltpu.roll(x, HEAD_DIM // 2, 1) * sine[span]).astype(jnp.bfloat16)

    def swap(g):
        span = pl.ds(*GROUPS[g])
        kv_own[span] = total[span, q_cols:].astype(jnp.bfloat16)
        copy = remote(
            kv_own.at[span, give], kv_in.at[span], kv_send.at[g], kv_recv.at[g], {"tp": across}
        )
        copy.start()
        kv_copies.append(copy)

    def attend(g):
        first, size = GROUPS[g]
        span = pl.ds(first, size)
        turned = [
            turn(total[span, h * HEAD_DIM : (h + 1) * HEAD_DIM], span)
            for h in range(q_cols // HEAD_DIM)
        ]
        reach = first + size
        row = lax.broadcasted_iota(jnp.int32, (size, reach), 0) + first
        column = lax.broadcasted_iota(jnp.int32, (size, reach), 1)
        allowed = (column <= row) & (column < length)
        live = lax.broadcasted_iota(jnp.int32, (size, HEAD_DIM), 0) + first < length
        kv_copies[g].wait_recv()
        kept = kv_own[span, keep]
        came = kv_in[span]
        first_side = jnp.full(kept.shape, tp, jnp.int32) == 0
        key = jnp.where(first_side, kept.astype(jnp.float32), came.astype(jnp.float32))
        value = jnp.where(first_side, came.astype(jnp.float32), kept.astype(jnp.float32))
        key_parts.append(turn(key, span))
        value_parts.append(value.astype(jnp.bfloat16))
        keys = jnp.concatenate(key_parts, axis=0)
        values = jnp.concatenate(value_parts, axis=0)
        for h, query in enumerate(turned):
            scores = lax.dot_general(
                query, keys, (((1,), (1,)), ((), ())), preferred_element_type=jnp.float32
            )
            scores = jnp.where(allowed, scores * scale, -jnp.inf)
            expo = jnp.exp(scores - jnp.max(scores, axis=1, keepdims=True))
            share_of = 1.0 / jnp.sum(expo, axis=1, keepdims=True)
            weights = (expo * share_of).astype(jnp.bfloat16)
            mixed = jnp.dot(weights, values, preferred_element_type=jnp.float32)
            out[span, h * HEAD_DIM : (h + 1) * HEAD_DIM] = jnp.where(live, mixed, 0.0).astype(
                jnp.bfloat16
            )

    swap(0)
    total[:, :q_cols] += 0.5 * jnp.dot(
        mid[:, :rank], up[:, :q_cols], preferred_element_type=jnp.float32
    )
    st_copies[PIECES - 1].wait_recv()
    add_piece(PIECES - 1, slice(q_cols, None))
    swap(1)
    add_piece(PIECES - 1, slice(0, q_cols))
    attend(0)
    attend(1)

    for copy in id_copies + st_copies + y_copies + c_copies + f_copies + [mid_copy] + kv_copies:
        copy.wait_send()
    for sent in z_copies:
        for copy in sent:
            copy.wait_send()


def tables(tokens):
    half = HEAD_DIM // 2
    position = np.arange(tokens, dtype=np.float32)
    inverse = np.float32(rope_base) ** (-(np.arange(half, dtype=np.float32) * 2.0) / HEAD_DIM).astype(
        np.float32
    )
    angle = position[:, None] * inverse[None, :].astype(np.float32)
    cosine = np.cos(angle)
    sine = np.sin(angle)
    return np.stack(
        [np.concatenate([cosine, cosine], axis=1), np.concatenate([-sine, sine], axis=1)]
    ).astype(np.float32)


def local_fused(
    planes,
    states,
    query_weight,
    key_value_weight,
    lengths,
    adapter_ids,
    adapter_slot,
    down_store,
    query_up_store,
    key_value_store,
):
    tokens, half = states.shape
    q_cols = query_weight.shape[1]
    kv_cols = key_value_weight.shape[1]
    cols = q_cols + kv_cols
    mine, rank = query_up_store.shape[:2]
    down_rows = jnp.transpose(down_store, (0, 2, 1))
    parts = 3
    lanes = half // parts
    trig = tables(tokens)
    peers = planes - 1
    vmem = pl.BlockSpec(memory_space=pltpu.VMEM)
    smem = pl.BlockSpec(memory_space=pltpu.SMEM)
    hbm = pl.BlockSpec(memory_space=pl.ANY)
    bf16, f32 = jnp.bfloat16, jnp.float32
    dma = pltpu.SemaphoreType.DMA
    return pl.pallas_call(
        functools.partial(fused, planes),
        out_shape=jax.ShapeDtypeStruct((tokens, q_cols), bf16),
        in_specs=[smem] * 3 + [hbm] * 7,
        out_specs=vmem,
        scratch_shapes=[
            pltpu.VMEM((tokens, half), bf16),
            pltpu.VMEM((tokens, half), bf16),
            pltpu.VMEM((half, cols), bf16),
            pltpu.VMEM((half, cols), bf16),
            pltpu.VMEM((tokens, cols), f32),
            pltpu.VMEM((4 * mine, 2 * rank, half), bf16),
            pltpu.VMEM((4 * mine, rank, cols), bf16),
            pltpu.VMEM((tokens, HEAD_DIM), f32),
            pltpu.VMEM((tokens, HEAD_DIM), f32),
            pltpu.VMEM((16, 128), jnp.int32),
            pltpu.VMEM((peers, 16, 128), jnp.int32),
            pltpu.VMEM((planes, 4 * mine, 16, 128), bf16),
            pltpu.VMEM((parts, peers, 2 * rank, lanes), bf16),
            pltpu.VMEM((peers, rank, cols), bf16),
            pltpu.VMEM((parts, peers, 2 * rank, lanes), bf16),
            pltpu.VMEM((peers, rank, cols), bf16),
            pltpu.VMEM((2 * rank, tokens), f32),
            pltpu.VMEM((2 * rank, tokens), f32),
            pltpu.VMEM((tokens, kv_cols), bf16),
            pltpu.VMEM((tokens, HEAD_DIM), bf16),
            dma((10,)),
            dma((PIECES,)),
            dma((PIECES,)),
            dma((parts + 2,)),
            dma((parts + 2,)),
            dma((parts + 2,)),
            dma((parts + 2,)),
            dma((parts + 1,)),
            dma((parts + 1,)),
            dma((peers,)),
            dma((peers,)),
            dma((parts + 1, peers)),
            dma((parts + 1, peers)),
            dma((1,)),
            dma((1,)),
            dma((len(GROUPS),)),
            dma((len(GROUPS),)),
        ],
        compiler_params=pltpu.CompilerParams(
            collective_id=0, has_side_effects=True, vmem_limit_bytes=60 * 1024 * 1024
        ),
        name="fused_attention",
    )(
        adapter_ids,
        adapter_slot,
        lengths,
        states,
        query_weight,
        key_value_weight,
        down_rows,
        query_up_store,
        key_value_store,
        trig,
    )


def solution(mesh):
    planes = mesh.shape["req"] // 4
    if mesh.shape["tp"] == 2 and planes == 4:
        body = functools.partial(local_fused, planes)
    else:
        body = local
    return jax.shard_map(
        body,
        mesh=mesh,
        in_specs=(
            P("req", "tp"),
            P(None, "tp"),
            P(None, "tp"),
            P("req"),
            P("req"),
            P(),
            P("req", "tp", None),
            P("req", None, "tp"),
            P("req", None, "tp"),
        ),
        out_specs=P("req", "tp"),
        check_vma=False,
    )
```

```python
import functools
import math

import jax
import jax.numpy as jnp
import numpy as np
from jax import lax
from jax.experimental import pallas as pl
from jax.experimental.pallas import tpu as pltpu
from jax.sharding import PartitionSpec as P

HEADS = 12
HEAD_DIM = 128


adapter_scale = 0.5
rope_base = 100000000000.0


def rotate(field):
    half = field.shape[-1] // 2
    count = field.shape[-3]
    position = jnp.arange(count).astype(jnp.float32)
    inverse = rope_base ** (-(jnp.arange(half).astype(jnp.float32) * 2.0) / field.shape[-1])
    angle = position[:, None] * inverse[None, :]
    cosine = jnp.cos(angle)[:, None, :]
    sine = jnp.sin(angle)[:, None, :]
    first_half = field[..., :half]
    second_half = field[..., half:]
    return jnp.concatenate(
        [first_half * cosine - second_half * sine, second_half * cosine + first_half * sine],
        axis=-1,
    )


def lookup_slots(wanted, adapter_slot):
    table = jnp.arange(adapter_slot.shape[0], dtype=jnp.int32)
    matches = wanted[:, None] == table[None, :]
    return jnp.sum(jnp.where(matches, adapter_slot[None, :], 0), axis=1)


def local(
    states,
    query_weight,
    key_value_weight,
    lengths,
    adapter_ids,
    adapter_slot,
    down_store,
    query_up_store,
    key_value_store,
):
    tp_index = lax.axis_index("tp")
    req_dev = lengths.shape[0]
    rows_total = states.shape[0]
    slot_len = rows_total // req_dev
    q_cols = query_weight.shape[1]
    kv_cols = key_value_weight.shape[1]
    heads_here = q_cols // HEAD_DIM
    pooled = (
        lax.all_gather(down_store, "req", axis=0, tiled=True),
        lax.all_gather(query_up_store, "req", axis=0, tiled=True),
        lax.all_gather(key_value_store, "req", axis=0, tiled=True),
    )
    own_slots = lookup_slots(adapter_ids, adapter_slot)
    adapter_down, adapter_query, adapter_pair = (
        jnp.take(member, own_slots, axis=0) for member in pooled
    )
    full_down = lax.all_gather(adapter_down, "tp", axis=1, tiled=True)
    piece = lax.all_gather(states, "tp", axis=1, tiled=True)
    width = piece.shape[1]
    grouped = piece.reshape(req_dev, slot_len, width)
    query_total = jnp.dot(piece, query_weight, preferred_element_type=jnp.float32)
    key_value_sum = jnp.dot(piece, key_value_weight, preferred_element_type=jnp.float32)
    rank_sum = jnp.einsum("rsd,rdk->rsk", grouped, full_down, preferred_element_type=jnp.float32)
    rank_mid = rank_sum.astype(jnp.bfloat16)
    rank_cols = rank_mid.shape[2] // 2
    query_addition = jnp.einsum(
        "rsk,rkc->rsc",
        rank_mid[:, :, :rank_cols],
        adapter_query,
        preferred_element_type=jnp.float32,
    ).reshape(rows_total, q_cols)
    key_value_extra = jnp.einsum(
        "rsk,rkc->rsc", rank_mid[:, :, rank_cols:], adapter_pair, preferred_element_type=jnp.float32
    ).reshape(rows_total, kv_cols)
    query_plain = query_total + adapter_scale * query_addition
    key_value_own = (key_value_sum + adapter_scale * key_value_extra).astype(jnp.bfloat16)
    pair_all = lax.all_gather(key_value_own, "tp", axis=1, tiled=True)
    key_width = pair_all.shape[1] // 2
    kv_heads = key_width // HEAD_DIM
    group = HEADS // kv_heads
    kv_index = tp_index * heads_here // group
    key_block = lax.dynamic_slice_in_dim(pair_all, kv_index * HEAD_DIM, HEAD_DIM, 1)
    value_block = lax.dynamic_slice_in_dim(pair_all, key_width + kv_index * HEAD_DIM, HEAD_DIM, 1)
    queries = rotate(query_plain.reshape(req_dev, slot_len, heads_here, HEAD_DIM)).astype(
        jnp.bfloat16
    )
    keys_one = rotate(key_block.astype(jnp.float32).reshape(req_dev, slot_len, 1, HEAD_DIM)).astype(
        jnp.bfloat16
    )[:, :, 0, :]
    values_one = value_block.reshape(req_dev, slot_len, HEAD_DIM)
    scale = 1.0 / math.sqrt(HEAD_DIM)
    scores = (
        jnp.einsum("rqhd,rkd->rhqk", queries, keys_one, preferred_element_type=jnp.float32) * scale
    )
    position = jnp.arange(slot_len, dtype=jnp.int32)
    allowed = (position[None, None, :] <= position[None, :, None]) & (
        position[None, None, :] < lengths[:, None, None]
    )
    scores = jnp.where(allowed[:, None, :, :], scores, -jnp.inf)
    highest = jnp.max(scores, axis=-1, keepdims=True)
    expo = jnp.exp(scores - highest)
    weights = (expo / jnp.sum(expo, axis=-1, keepdims=True)).astype(jnp.bfloat16)
    context = jnp.einsum("rhqk,rkd->rqhd", weights, values_one, preferred_element_type=jnp.float32)
    live_rows = position[None, :] < lengths[:, None]
    context = jnp.where(live_rows[:, :, None, None], context, 0.0)
    return context.reshape(rows_total, q_cols).astype(jnp.bfloat16)


MESH = pl.DeviceIdType.MESH
PIECES = 4
GROUPS = ((0, 192), (192, 64))


def fused(
    planes,
    ids,
    slots,
    lengths,
    states,
    wq,
    wkv,
    down_rows,
    query_rows,
    pair_rows,
    trig,
    out,
    own_st,
    other_st,
    wq_own,
    wkv_own,
    wq_other,
    wkv_other,
    total,
    plane_down,
    plane_q,
    plane_kv,
    turns,
    ids_own,
    ids_in,
    flags,
    leave_down,
    leave_kv,
    leave_q,
    land_down,
    land_kv,
    land_q,
    mid_out,
    mid_in,
    kv_own,
    kv_in,
    local_sem,
    st_send,
    st_recv,
    y_send,
    y_recv,
    c_send,
    c_recv,
    f_send,
    f_recv,
    i_send,
    i_recv,
    z_send,
    z_recv,
    m_send,
    m_recv,
    kv_send,
    kv_recv,
):
    r = lax.axis_index("req")
    tp = lax.axis_index("tp")
    per_plane = 4
    count = planes * per_plane
    half = own_st.shape[1]
    q_cols = wq.shape[1]
    tokens = own_st.shape[0]
    step = tokens // PIECES
    parts = plane_down.shape[0]
    mine, rank = plane_q.shape[0] // per_plane, plane_q.shape[1]
    core_peer = r + 1 - 2 * (r % 2)
    y_peer = r + 2 - 4 * ((r // 2) % 2)
    z_peers = [(r + per_plane * d) % count for d in range(1, planes)]
    across = 1 - tp
    base = (r // per_plane) * (per_plane * mine)

    def place(index):
        return pl.ds((index % per_plane) * mine, mine)

    def remote(src, dst, send, recv, who):
        return pltpu.make_async_remote_copy(
            src_ref=src, dst_ref=dst, send_sem=send, recv_sem=recv, device_id=who, device_id_type=MESH
        )

    own_rows = pl.ds(pl.multiple_of(tp * half, half), half)
    other_rows = pl.ds(pl.multiple_of(across * half, half), half)
    loads = [
        pltpu.make_async_copy(states, own_st, local_sem.at[0]),
        pltpu.make_async_copy(wq.at[own_rows], wq_own, local_sem.at[1]),
        pltpu.make_async_copy(wkv.at[own_rows], wkv_own, local_sem.at[2]),
        pltpu.make_async_copy(wq.at[other_rows], wq_other, local_sem.at[3]),
        pltpu.make_async_copy(wkv.at[other_rows], wkv_other, local_sem.at[4]),
        pltpu.make_async_copy(trig, turns, local_sem.at[5]),
        pltpu.make_async_copy(query_rows, plane_q.at[place(r)], local_sem.at[6]),
        pltpu.make_async_copy(pair_rows, plane_kv.at[place(r)], local_sem.at[7]),
    ] + [
        pltpu.make_async_copy(
            down_rows.at[:, pl.ds(k * rank, rank)], plane_down.at[k, place(r)], local_sem.at[8 + k]
        )
        for k in range(parts)
    ]
    for copy in loads:
        copy.start()

    ids_own[...] = jnp.full(ids_own.shape, slots[ids[0]], jnp.int32)

    barrier = pltpu.get_barrier_semaphore()
    for peer in [core_peer, y_peer] + z_peers:
        pl.semaphore_signal(barrier, inc=1, device_id={"req": peer}, device_id_type=MESH)
    pl.semaphore_signal(barrier, inc=1, device_id={"tp": across}, device_id_type=MESH)
    pl.semaphore_wait(barrier, planes + 2)

    id_copies = [
        remote(ids_own, ids_in.at[d], i_send.at[d], i_recv.at[d], {"req": peer})
        for d, peer in enumerate(z_peers)
    ]
    st_copies = [
        remote(
            states.at[pl.ds(p * step, step)],
            other_st.at[pl.ds(p * step, step)],
            st_send.at[p],
            st_recv.at[p],
            {"tp": across},
        )
        for p in range(PIECES)
    ]
    def share(peer, send, recv):
        ends = [
            (down_rows.at[:, pl.ds(k * rank, rank)], plane_down.at[k, place(r)]) for k in range(parts)
        ] + [(pair_rows, plane_kv.at[place(r)]), (query_rows, plane_q.at[place(r)])]
        return [
            remote(source, target, send.at[n], recv.at[n], {"req": peer})
            for n, (source, target) in enumerate(ends)
        ]

    planes_of = [plane_down.at[k] for k in range(parts)] + [plane_kv, plane_q]
    leaves = [leave_down.at[k] for k in range(parts)] + [leave_kv, leave_q]
    lands = [land_down.at[k] for k in range(parts)] + [land_kv, land_q]
    y_copies = share(y_peer, y_send, y_recv)
    c_copies = share(core_peer, c_send, c_recv)
    f_copies = [
        remote(
            block.at[place(y_peer)],
            block.at[place(y_peer)],
            f_send.at[k],
            f_recv.at[k],
            {"req": core_peer},
        )
        for k, block in enumerate(planes_of)
    ]
    y_copies[0].start()
    st_copies[0].start()
    for copy in id_copies + y_copies[1:] + c_copies + st_copies[1:]:
        copy.start()

    for n in (0, 1, 2):
        loads[n].wait()
    total[:, :q_cols] = jnp.dot(own_st[...], wq_own[...], preferred_element_type=jnp.float32)
    total[:, q_cols:] = jnp.dot(own_st[...], wkv_own[...], preferred_element_type=jnp.float32)
    for copy in loads[3:]:
        copy.wait()
    for copy in id_copies:
        copy.wait_recv()

    def add_q(p):
        span = pl.ds(p * step, step)
        total[span, :q_cols] += jnp.dot(
            other_st[span], wq_other[...], preferred_element_type=jnp.float32
        )

    def add_kv(p):
        span = pl.ds(p * step, step)
        total[span, q_cols:] += jnp.dot(
            other_st[span], wkv_other[...], preferred_element_type=jnp.float32
        )

    def add_piece(p):
        st_copies[p].wait_recv()
        add_kv(p)
        add_q(p)

    z_copies = []

    for d in range(planes):
        wanted = ids_own[...] if d == 0 else ids_in[planes - 1 - d]
        for j in range(per_plane * mine):
            flags[d, j] = jnp.where(wanted == base + j, 1.0, 0.0).astype(jnp.bfloat16)

    def forward(k):
        y_copies[k].wait_recv()
        f_copies[k].start()

    def stage(k):
        c_copies[k].wait_recv()
        f_copies[k].wait_recv()
        source, leave, land = planes_of[k], leaves[k], lands[k]
        sums = [None] * planes
        for j in range(per_plane * mine):
            record = source[j]
            for d in range(planes):
                flag = jnp.concatenate([flags[d, j]] * (record.shape[1] // flags.shape[3]), axis=1)
                sums[d] = flag * record if j == 0 else sums[d] + flag * record
        for d in range(1, planes):
            leave[d - 1] = sums[d]
        sent = [
            remote(leave.at[d], land.at[d], z_send.at[k, d], z_recv.at[k, d], {"req": peer})
            for d, peer in enumerate(z_peers)
        ]
        for copy in sent:
            copy.start()
        z_copies.append(sent)
        return sums[0]

    def take(k):
        for copy in z_copies[k]:
            copy.wait_recv()
        record = held[k]
        for d in range(planes - 1):
            record = record + lands[k][d]
        return record

    def lower(k):
        mid_out[k * rank : (k + 1) * rank] = lax.dot_general(
            take(k), own_st[...], (((1,), (1,)), ((), ())), preferred_element_type=jnp.float32
        )

    held = []
    forward(0)
    held.append(stage(0))
    forward(1)
    held.append(stage(1))
    lower(0)
    add_piece(0)
    forward(2)
    forward(3)
    held.append(stage(2))
    held.append(stage(3))
    lower(1)
    mid_copy = remote(mid_out, mid_in, m_send.at[0], m_recv.at[0], {"tp": across})
    mid_copy.start()
    for p in range(1, PIECES - 1):
        add_piece(p)
    mid_copy.wait_recv()
    mid = jnp.transpose(mid_out[...] + mid_in[...]).astype(jnp.bfloat16)
    total[:, q_cols:] += 0.5 * jnp.dot(mid[:, rank:], take(2), preferred_element_type=jnp.float32)

    keep = pl.ds(pl.multiple_of(tp * HEAD_DIM, HEAD_DIM), HEAD_DIM)
    give = pl.ds(pl.multiple_of(across * HEAD_DIM, HEAD_DIM), HEAD_DIM)
    scale = 1.0 / math.sqrt(HEAD_DIM)
    length = lengths[0]
    kv_copies = []
    key_parts = []
    value_parts = []

    def turn(x, span):
        return (x * turns[0, span] + pltpu.roll(x, HEAD_DIM // 2, 1) * turns[1, span]).astype(jnp.bfloat16)

    def swap(g):
        span = pl.ds(*GROUPS[g])
        kv_own[span] = total[span, q_cols:].astype(jnp.bfloat16)
        copy = remote(
            kv_own.at[span, give], kv_in.at[span], kv_send.at[g], kv_recv.at[g], {"tp": across}
        )
        copy.start()
        kv_copies.append(copy)

    def attend(g):
        first, size = GROUPS[g]
        span = pl.ds(first, size)
        turned = [
            turn(total[span, h * HEAD_DIM : (h + 1) * HEAD_DIM], span)
            for h in range(q_cols // HEAD_DIM)
        ]
        reach = first + size
        row = lax.broadcasted_iota(jnp.int32, (size, reach), 0) + first
        column = lax.broadcasted_iota(jnp.int32, (size, reach), 1)
        allowed = (column <= row) & (column < length)
        live = lax.broadcasted_iota(jnp.int32, (size, HEAD_DIM), 0) + first < length
        kv_copies[g].wait_recv()
        kept = kv_own[span, keep]
        came = kv_in[span]
        first_side = jnp.full(kept.shape, tp, jnp.int32) == 0
        key = jnp.where(first_side, kept.astype(jnp.float32), came.astype(jnp.float32))
        value = jnp.where(first_side, came.astype(jnp.float32), kept.astype(jnp.float32))
        key_parts.append(turn(key, span))
        value_parts.append(value.astype(jnp.bfloat16))
        keys = jnp.concatenate(key_parts, axis=0)
        values = jnp.concatenate(value_parts, axis=0)
        for h, query in enumerate(turned):
            scores = lax.dot_general(
                query, keys, (((1,), (1,)), ((), ())), preferred_element_type=jnp.float32
            )
            scores = jnp.where(allowed, scores * scale, -jnp.inf)
            expo = jnp.exp(scores - jnp.max(scores, axis=1, keepdims=True))
            share_of = 1.0 / jnp.sum(expo, axis=1, keepdims=True)
            weights = (expo * share_of).astype(jnp.bfloat16)
            mixed = jnp.dot(weights, values, preferred_element_type=jnp.float32)
            out[span, h * HEAD_DIM : (h + 1) * HEAD_DIM] = jnp.where(live, mixed, 0.0).astype(
                jnp.bfloat16
            )

    swap(0)
    total[:, :q_cols] += 0.5 * jnp.dot(
        mid[:, :rank], take(3), preferred_element_type=jnp.float32
    )
    st_copies[PIECES - 1].wait_recv()
    add_kv(PIECES - 1)
    swap(1)
    add_q(PIECES - 1)
    attend(0)
    attend(1)

    for copy in id_copies + st_copies + y_copies + c_copies + f_copies + [mid_copy] + kv_copies:
        copy.wait_send()
    for sent in z_copies:
        for copy in sent:
            copy.wait_send()


def tables(tokens):
    half = HEAD_DIM // 2
    position = np.arange(tokens, dtype=np.float32)
    inverse = np.float32(rope_base) ** (-(np.arange(half, dtype=np.float32) * 2.0) / HEAD_DIM).astype(
        np.float32
    )
    angle = position[:, None] * inverse[None, :].astype(np.float32)
    cosine = np.cos(angle)
    sine = np.sin(angle)
    return np.stack(
        [np.concatenate([cosine, cosine], axis=1), np.concatenate([-sine, sine], axis=1)]
    ).astype(np.float32)


def local_fused(
    planes,
    states,
    query_weight,
    key_value_weight,
    lengths,
    adapter_ids,
    adapter_slot,
    down_store,
    query_up_store,
    key_value_store,
):
    tokens, half = states.shape
    q_cols = query_weight.shape[1]
    kv_cols = key_value_weight.shape[1]
    cols = q_cols + kv_cols
    mine, rank = query_up_store.shape[:2]
    down_rows = jnp.transpose(down_store, (0, 2, 1))
    parts = 2
    trig = tables(tokens)
    peers = planes - 1
    vmem = pl.BlockSpec(memory_space=pltpu.VMEM)
    smem = pl.BlockSpec(memory_space=pltpu.SMEM)
    hbm = pl.BlockSpec(memory_space=pl.ANY)
    bf16, f32 = jnp.bfloat16, jnp.float32
    dma = pltpu.SemaphoreType.DMA
    return pl.pallas_call(
        functools.partial(fused, planes),
        out_shape=jax.ShapeDtypeStruct((tokens, q_cols), bf16),
        in_specs=[smem] * 3 + [hbm] * 7,
        out_specs=vmem,
        scratch_shapes=[
            pltpu.VMEM((tokens, half), bf16),
            pltpu.VMEM((tokens, half), bf16),
            pltpu.VMEM((half, q_cols), bf16),
            pltpu.VMEM((half, kv_cols), bf16),
            pltpu.VMEM((half, q_cols), bf16),
            pltpu.VMEM((half, kv_cols), bf16),
            pltpu.VMEM((tokens, cols), f32),
            pltpu.VMEM((parts, 4 * mine, rank, half), bf16),
            pltpu.VMEM((4 * mine, rank, q_cols), bf16),
            pltpu.VMEM((4 * mine, rank, kv_cols), bf16),
            pltpu.VMEM(trig.shape, f32),
            pltpu.VMEM((16, 128), jnp.int32),
            pltpu.VMEM((peers, 16, 128), jnp.int32),
            pltpu.VMEM((planes, 4 * mine, 16, 128), bf16),
            pltpu.VMEM((parts, peers, rank, half), bf16),
            pltpu.VMEM((peers, rank, kv_cols), bf16),
            pltpu.VMEM((peers, rank, q_cols), bf16),
            pltpu.VMEM((parts, peers, rank, half), bf16),
            pltpu.VMEM((peers, rank, kv_cols), bf16),
            pltpu.VMEM((peers, rank, q_cols), bf16),
            pltpu.VMEM((2 * rank, tokens), f32),
            pltpu.VMEM((2 * rank, tokens), f32),
            pltpu.VMEM((tokens, kv_cols), bf16),
            pltpu.VMEM((tokens, HEAD_DIM), bf16),
            dma((10,)),
            dma((PIECES,)),
            dma((PIECES,)),
            dma((parts + 2,)),
            dma((parts + 2,)),
            dma((parts + 2,)),
            dma((parts + 2,)),
            dma((parts + 2,)),
            dma((parts + 2,)),
            dma((peers,)),
            dma((peers,)),
            dma((parts + 2, peers)),
            dma((parts + 2, peers)),
            dma((1,)),
            dma((1,)),
            dma((len(GROUPS),)),
            dma((len(GROUPS),)),
        ],
        compiler_params=pltpu.CompilerParams(
            collective_id=0, has_side_effects=True, vmem_limit_bytes=60 * 1024 * 1024
        ),
        name="fused_attention",
    )(
        adapter_ids,
        adapter_slot,
        lengths,
        states,
        query_weight,
        key_value_weight,
        down_rows,
        query_up_store,
        key_value_store,
        trig,
    )


def solution(mesh):
    planes = mesh.shape["req"] // 4
    if mesh.shape["tp"] == 2 and planes == 4:
        body = functools.partial(local_fused, planes)
    else:
        body = local
    return jax.shard_map(
        body,
        mesh=mesh,
        in_specs=(
            P("req", "tp"),
            P(None, "tp"),
            P(None, "tp"),
            P("req"),
            P("req"),
            P(),
            P("req", "tp", None),
            P("req", None, "tp"),
            P("req", None, "tp"),
        ),
        out_specs=P("req", "tp"),
        check_vma=False,
    )
```

```python
import functools
import math

import jax
import jax.numpy as jnp
import numpy as np
from jax import lax
from jax.experimental import pallas as pl
from jax.experimental.pallas import tpu as pltpu
from jax.sharding import PartitionSpec as P

HEADS = 12
HEAD_DIM = 128


adapter_scale = 0.5
rope_base = 100000000000.0


def rotate(field):
    half = field.shape[-1] // 2
    count = field.shape[-3]
    position = jnp.arange(count).astype(jnp.float32)
    inverse = rope_base ** (-(jnp.arange(half).astype(jnp.float32) * 2.0) / field.shape[-1])
    angle = position[:, None] * inverse[None, :]
    cosine = jnp.cos(angle)[:, None, :]
    sine = jnp.sin(angle)[:, None, :]
    first_half = field[..., :half]
    second_half = field[..., half:]
    return jnp.concatenate(
        [first_half * cosine - second_half * sine, second_half * cosine + first_half * sine],
        axis=-1,
    )


def lookup_slots(wanted, adapter_slot):
    table = jnp.arange(adapter_slot.shape[0], dtype=jnp.int32)
    matches = wanted[:, None] == table[None, :]
    return jnp.sum(jnp.where(matches, adapter_slot[None, :], 0), axis=1)


def local(
    states,
    query_weight,
    key_value_weight,
    lengths,
    adapter_ids,
    adapter_slot,
    down_store,
    query_up_store,
    key_value_store,
):
    tp_index = lax.axis_index("tp")
    req_dev = lengths.shape[0]
    rows_total = states.shape[0]
    slot_len = rows_total // req_dev
    q_cols = query_weight.shape[1]
    kv_cols = key_value_weight.shape[1]
    heads_here = q_cols // HEAD_DIM
    pooled = (
        lax.all_gather(down_store, "req", axis=0, tiled=True),
        lax.all_gather(query_up_store, "req", axis=0, tiled=True),
        lax.all_gather(key_value_store, "req", axis=0, tiled=True),
    )
    own_slots = lookup_slots(adapter_ids, adapter_slot)
    adapter_down, adapter_query, adapter_pair = (
        jnp.take(member, own_slots, axis=0) for member in pooled
    )
    full_down = lax.all_gather(adapter_down, "tp", axis=1, tiled=True)
    piece = lax.all_gather(states, "tp", axis=1, tiled=True)
    width = piece.shape[1]
    grouped = piece.reshape(req_dev, slot_len, width)
    query_total = jnp.dot(piece, query_weight, preferred_element_type=jnp.float32)
    key_value_sum = jnp.dot(piece, key_value_weight, preferred_element_type=jnp.float32)
    rank_sum = jnp.einsum("rsd,rdk->rsk", grouped, full_down, preferred_element_type=jnp.float32)
    rank_mid = rank_sum.astype(jnp.bfloat16)
    rank_cols = rank_mid.shape[2] // 2
    query_addition = jnp.einsum(
        "rsk,rkc->rsc",
        rank_mid[:, :, :rank_cols],
        adapter_query,
        preferred_element_type=jnp.float32,
    ).reshape(rows_total, q_cols)
    key_value_extra = jnp.einsum(
        "rsk,rkc->rsc", rank_mid[:, :, rank_cols:], adapter_pair, preferred_element_type=jnp.float32
    ).reshape(rows_total, kv_cols)
    query_plain = query_total + adapter_scale * query_addition
    key_value_own = (key_value_sum + adapter_scale * key_value_extra).astype(jnp.bfloat16)
    pair_all = lax.all_gather(key_value_own, "tp", axis=1, tiled=True)
    key_width = pair_all.shape[1] // 2
    kv_heads = key_width // HEAD_DIM
    group = HEADS // kv_heads
    kv_index = tp_index * heads_here // group
    key_block = lax.dynamic_slice_in_dim(pair_all, kv_index * HEAD_DIM, HEAD_DIM, 1)
    value_block = lax.dynamic_slice_in_dim(pair_all, key_width + kv_index * HEAD_DIM, HEAD_DIM, 1)
    queries = rotate(query_plain.reshape(req_dev, slot_len, heads_here, HEAD_DIM)).astype(
        jnp.bfloat16
    )
    keys_one = rotate(key_block.astype(jnp.float32).reshape(req_dev, slot_len, 1, HEAD_DIM)).astype(
        jnp.bfloat16
    )[:, :, 0, :]
    values_one = value_block.reshape(req_dev, slot_len, HEAD_DIM)
    scale = 1.0 / math.sqrt(HEAD_DIM)
    scores = (
        jnp.einsum("rqhd,rkd->rhqk", queries, keys_one, preferred_element_type=jnp.float32) * scale
    )
    position = jnp.arange(slot_len, dtype=jnp.int32)
    allowed = (position[None, None, :] <= position[None, :, None]) & (
        position[None, None, :] < lengths[:, None, None]
    )
    scores = jnp.where(allowed[:, None, :, :], scores, -jnp.inf)
    highest = jnp.max(scores, axis=-1, keepdims=True)
    expo = jnp.exp(scores - highest)
    weights = (expo / jnp.sum(expo, axis=-1, keepdims=True)).astype(jnp.bfloat16)
    context = jnp.einsum("rhqk,rkd->rqhd", weights, values_one, preferred_element_type=jnp.float32)
    live_rows = position[None, :] < lengths[:, None]
    context = jnp.where(live_rows[:, :, None, None], context, 0.0)
    return context.reshape(rows_total, q_cols).astype(jnp.bfloat16)


MESH = pl.DeviceIdType.MESH
PIECES = 4
GROUPS = ((0, 192), (192, 64))


def fused(
    planes,
    ids,
    slots,
    lengths,
    states,
    wq,
    wkv,
    down_rows,
    query_rows,
    pair_rows,
    trig,
    out,
    own_st,
    other_st,
    wq_own,
    wkv_own,
    wq_other,
    wkv_other,
    total,
    plane_down,
    plane_q,
    plane_kv,
    turns,
    ids_own,
    ids_in,
    flags,
    leave_down,
    leave_kv,
    leave_q,
    land_down,
    land_kv,
    land_q,
    mid_out,
    mid_in,
    kv_own,
    kv_in,
    local_sem,
    st_send,
    st_recv,
    y_send,
    y_recv,
    c_send,
    c_recv,
    f_send,
    f_recv,
    i_send,
    i_recv,
    z_send,
    z_recv,
    m_send,
    m_recv,
    kv_send,
    kv_recv,
):
    r = lax.axis_index("req")
    tp = lax.axis_index("tp")
    per_plane = 4
    count = planes * per_plane
    half = own_st.shape[1]
    q_cols = wq.shape[1]
    tokens = own_st.shape[0]
    step = tokens // PIECES
    parts = plane_down.shape[0]
    mine, rank = plane_q.shape[0] // per_plane, plane_q.shape[1]
    core_peer = r + 1 - 2 * (r % 2)
    y_peer = r + 2 - 4 * ((r // 2) % 2)
    z_peers = [(r + per_plane * d) % count for d in range(1, planes)]
    across = 1 - tp
    base = (r // per_plane) * (per_plane * mine)

    def place(index):
        return pl.ds((index % per_plane) * mine, mine)

    def remote(src, dst, send, recv, who):
        return pltpu.make_async_remote_copy(
            src_ref=src, dst_ref=dst, send_sem=send, recv_sem=recv, device_id=who, device_id_type=MESH
        )

    own_rows = pl.ds(pl.multiple_of(tp * half, half), half)
    other_rows = pl.ds(pl.multiple_of(across * half, half), half)
    loads = [
        pltpu.make_async_copy(states, own_st, local_sem.at[0]),
        pltpu.make_async_copy(wq.at[own_rows], wq_own, local_sem.at[1]),
        pltpu.make_async_copy(wkv.at[own_rows], wkv_own, local_sem.at[2]),
        pltpu.make_async_copy(wq.at[other_rows], wq_other, local_sem.at[3]),
        pltpu.make_async_copy(wkv.at[other_rows], wkv_other, local_sem.at[4]),
        pltpu.make_async_copy(trig, turns, local_sem.at[5]),
        pltpu.make_async_copy(query_rows, plane_q.at[place(r)], local_sem.at[6]),
        pltpu.make_async_copy(pair_rows, plane_kv.at[place(r)], local_sem.at[7]),
    ] + [
        pltpu.make_async_copy(
            down_rows.at[:, pl.ds(k * rank, rank)], plane_down.at[k, place(r)], local_sem.at[8 + k]
        )
        for k in range(parts)
    ]
    for copy in loads:
        copy.start()

    ids_own[...] = jnp.full(ids_own.shape, slots[ids[0]], jnp.int32)

    barrier = pltpu.get_barrier_semaphore()
    for peer in [core_peer, y_peer] + z_peers:
        pl.semaphore_signal(barrier, inc=1, device_id={"req": peer}, device_id_type=MESH)
    pl.semaphore_signal(barrier, inc=1, device_id={"tp": across}, device_id_type=MESH)
    pl.semaphore_wait(barrier, planes + 2)

    id_copies = [
        remote(ids_own, ids_in.at[d], i_send.at[d], i_recv.at[d], {"req": peer})
        for d, peer in enumerate(z_peers)
    ]
    st_copies = [
        remote(
            states.at[pl.ds(p * step, step)],
            other_st.at[pl.ds(p * step, step)],
            st_send.at[p],
            st_recv.at[p],
            {"tp": across},
        )
        for p in range(PIECES)
    ]
    def share(peer, send, recv):
        ends = [
            (down_rows.at[:, pl.ds(k * rank, rank)], plane_down.at[k, place(r)]) for k in range(parts)
        ] + [(pair_rows, plane_kv.at[place(r)]), (query_rows, plane_q.at[place(r)])]
        return [
            remote(source, target, send.at[n], recv.at[n], {"req": peer})
            for n, (source, target) in enumerate(ends)
        ]

    planes_of = [plane_down.at[k] for k in range(parts)] + [plane_kv, plane_q]
    leaves = [leave_down.at[k] for k in range(parts)] + [leave_kv, leave_q]
    lands = [land_down.at[k] for k in range(parts)] + [land_kv, land_q]
    y_copies = share(y_peer, y_send, y_recv)
    c_copies = share(core_peer, c_send, c_recv)
    f_copies = [
        remote(
            block.at[place(y_peer)],
            block.at[place(y_peer)],
            f_send.at[k],
            f_recv.at[k],
            {"req": core_peer},
        )
        for k, block in enumerate(planes_of)
    ]
    def after(done, following):
        done.wait_send()
        for copy in following:
            copy.start()

    for copy in [y_copies[0], st_copies[0]] + id_copies + [c_copies[0]]:
        copy.start()

    for n in (0, 1, 2):
        loads[n].wait()
    total[:, :q_cols] = jnp.dot(own_st[...], wq_own[...], preferred_element_type=jnp.float32)
    total[:, q_cols:] = jnp.dot(own_st[...], wkv_own[...], preferred_element_type=jnp.float32)
    for copy in loads[3:]:
        copy.wait()
    for copy in id_copies:
        copy.wait_recv()

    def add_q(p):
        span = pl.ds(p * step, step)
        total[span, :q_cols] += jnp.dot(
            other_st[span], wq_other[...], preferred_element_type=jnp.float32
        )

    def add_kv(p):
        span = pl.ds(p * step, step)
        total[span, q_cols:] += jnp.dot(
            other_st[span], wkv_other[...], preferred_element_type=jnp.float32
        )

    def add_piece(p):
        st_copies[p].wait_recv()
        add_kv(p)
        add_q(p)

    z_copies = []

    for d in range(planes):
        wanted = ids_own[...] if d == 0 else ids_in[planes - 1 - d]
        for j in range(per_plane * mine):
            flags[d, j] = jnp.where(wanted == base + j, 1.0, 0.0).astype(jnp.bfloat16)

    def forward(k):
        y_copies[k].wait_recv()
        f_copies[k].start()

    def stage(k):
        c_copies[k].wait_recv()
        f_copies[k].wait_recv()
        source, leave, land = planes_of[k], leaves[k], lands[k]
        sums = [None] * planes
        for j in range(per_plane * mine):
            record = source[j]
            for d in range(planes):
                flag = jnp.concatenate([flags[d, j]] * (record.shape[1] // flags.shape[3]), axis=1)
                sums[d] = flag * record if j == 0 else sums[d] + flag * record
        for d in range(1, planes):
            leave[d - 1] = sums[d]
        sent = [
            remote(leave.at[d], land.at[d], z_send.at[k, d], z_recv.at[k, d], {"req": peer})
            for d, peer in enumerate(z_peers)
        ]
        for copy in sent:
            copy.start()
        z_copies.append(sent)
        return sums[0]

    def take(k):
        for copy in z_copies[k]:
            copy.wait_recv()
        record = held[k]
        for d in range(planes - 1):
            record = record + lands[k][d]
        return record

    def lower(k):
        mid_out[k * rank : (k + 1) * rank] = lax.dot_general(
            take(k), own_st[...], (((1,), (1,)), ((), ())), preferred_element_type=jnp.float32
        )

    held = []
    after(y_copies[0], [y_copies[1], c_copies[1]])
    after(st_copies[0], [st_copies[1]])
    forward(0)
    held.append(stage(0))
    add_piece(0)
    after(y_copies[1], y_copies[2:] + c_copies[2:])
    after(st_copies[1], [st_copies[2]])
    forward(1)
    held.append(stage(1))
    lower(0)
    add_piece(1)
    forward(2)
    forward(3)
    after(st_copies[2], [st_copies[3]])
    held.append(stage(2))
    held.append(stage(3))
    lower(1)
    mid_copy = remote(mid_out, mid_in, m_send.at[0], m_recv.at[0], {"tp": across})
    mid_copy.start()
    add_piece(2)
    mid_copy.wait_recv()
    mid = jnp.transpose(mid_out[...] + mid_in[...]).astype(jnp.bfloat16)
    total[:, q_cols:] += 0.5 * jnp.dot(mid[:, rank:], take(2), preferred_element_type=jnp.float32)

    keep = pl.ds(pl.multiple_of(tp * HEAD_DIM, HEAD_DIM), HEAD_DIM)
    give = pl.ds(pl.multiple_of(across * HEAD_DIM, HEAD_DIM), HEAD_DIM)
    scale = 1.0 / math.sqrt(HEAD_DIM)
    length = lengths[0]
    kv_copies = []
    key_parts = []
    value_parts = []

    def turn(x, span):
        return (x * turns[0, span] + pltpu.roll(x, HEAD_DIM // 2, 1) * turns[1, span]).astype(jnp.bfloat16)

    def swap(g):
        span = pl.ds(*GROUPS[g])
        kv_own[span] = total[span, q_cols:].astype(jnp.bfloat16)
        copy = remote(
            kv_own.at[span, give], kv_in.at[span], kv_send.at[g], kv_recv.at[g], {"tp": across}
        )
        copy.start()
        kv_copies.append(copy)

    def attend(g):
        first, size = GROUPS[g]
        span = pl.ds(first, size)
        turned = [
            turn(total[span, h * HEAD_DIM : (h + 1) * HEAD_DIM], span)
            for h in range(q_cols // HEAD_DIM)
        ]
        reach = first + size
        row = lax.broadcasted_iota(jnp.int32, (size, reach), 0) + first
        column = lax.broadcasted_iota(jnp.int32, (size, reach), 1)
        allowed = (column <= row) & (column < length)
        live = lax.broadcasted_iota(jnp.int32, (size, HEAD_DIM), 0) + first < length
        kv_copies[g].wait_recv()
        kept = kv_own[span, keep]
        came = kv_in[span]
        first_side = jnp.full(kept.shape, tp, jnp.int32) == 0
        key = jnp.where(first_side, kept.astype(jnp.float32), came.astype(jnp.float32))
        value = jnp.where(first_side, came.astype(jnp.float32), kept.astype(jnp.float32))
        key_parts.append(turn(key, span))
        value_parts.append(value.astype(jnp.bfloat16))
        keys = jnp.concatenate(key_parts, axis=0)
        values = jnp.concatenate(value_parts, axis=0)
        for h, query in enumerate(turned):
            scores = lax.dot_general(
                query, keys, (((1,), (1,)), ((), ())), preferred_element_type=jnp.float32
            )
            scores = jnp.where(allowed, scores * scale, -jnp.inf)
            expo = jnp.exp(scores - jnp.max(scores, axis=1, keepdims=True))
            share_of = 1.0 / jnp.sum(expo, axis=1, keepdims=True)
            weights = (expo * share_of).astype(jnp.bfloat16)
            mixed = jnp.dot(weights, values, preferred_element_type=jnp.float32)
            out[span, h * HEAD_DIM : (h + 1) * HEAD_DIM] = jnp.where(live, mixed, 0.0).astype(
                jnp.bfloat16
            )

    swap(0)
    total[:, :q_cols] += 0.5 * jnp.dot(
        mid[:, :rank], take(3), preferred_element_type=jnp.float32
    )
    st_copies[PIECES - 1].wait_recv()
    add_kv(PIECES - 1)
    swap(1)
    add_q(PIECES - 1)
    attend(0)
    attend(1)

    for copy in id_copies + st_copies[3:] + y_copies[2:] + c_copies + f_copies + [mid_copy] + kv_copies:
        copy.wait_send()
    for sent in z_copies:
        for copy in sent:
            copy.wait_send()


def tables(tokens):
    half = HEAD_DIM // 2
    position = np.arange(tokens, dtype=np.float32)
    inverse = np.float32(rope_base) ** (-(np.arange(half, dtype=np.float32) * 2.0) / HEAD_DIM).astype(
        np.float32
    )
    angle = position[:, None] * inverse[None, :].astype(np.float32)
    cosine = np.cos(angle)
    sine = np.sin(angle)
    return np.stack(
        [np.concatenate([cosine, cosine], axis=1), np.concatenate([-sine, sine], axis=1)]
    ).astype(np.float32)


def local_fused(
    planes,
    states,
    query_weight,
    key_value_weight,
    lengths,
    adapter_ids,
    adapter_slot,
    down_store,
    query_up_store,
    key_value_store,
):
    tokens, half = states.shape
    q_cols = query_weight.shape[1]
    kv_cols = key_value_weight.shape[1]
    cols = q_cols + kv_cols
    mine, rank = query_up_store.shape[:2]
    down_rows = jnp.transpose(down_store, (0, 2, 1))
    parts = 2
    trig = tables(tokens)
    peers = planes - 1
    vmem = pl.BlockSpec(memory_space=pltpu.VMEM)
    smem = pl.BlockSpec(memory_space=pltpu.SMEM)
    hbm = pl.BlockSpec(memory_space=pl.ANY)
    bf16, f32 = jnp.bfloat16, jnp.float32
    dma = pltpu.SemaphoreType.DMA
    return pl.pallas_call(
        functools.partial(fused, planes),
        out_shape=jax.ShapeDtypeStruct((tokens, q_cols), bf16),
        in_specs=[smem] * 3 + [hbm] * 7,
        out_specs=vmem,
        scratch_shapes=[
            pltpu.VMEM((tokens, half), bf16),
            pltpu.VMEM((tokens, half), bf16),
            pltpu.VMEM((half, q_cols), bf16),
            pltpu.VMEM((half, kv_cols), bf16),
            pltpu.VMEM((half, q_cols), bf16),
            pltpu.VMEM((half, kv_cols), bf16),
            pltpu.VMEM((tokens, cols), f32),
            pltpu.VMEM((parts, 4 * mine, rank, half), bf16),
            pltpu.VMEM((4 * mine, rank, q_cols), bf16),
            pltpu.VMEM((4 * mine, rank, kv_cols), bf16),
            pltpu.VMEM(trig.shape, f32),
            pltpu.VMEM((16, 128), jnp.int32),
            pltpu.VMEM((peers, 16, 128), jnp.int32),
            pltpu.VMEM((planes, 4 * mine, 16, 128), bf16),
            pltpu.VMEM((parts, peers, rank, half), bf16),
            pltpu.VMEM((peers, rank, kv_cols), bf16),
            pltpu.VMEM((peers, rank, q_cols), bf16),
            pltpu.VMEM((parts, peers, rank, half), bf16),
            pltpu.VMEM((peers, rank, kv_cols), bf16),
            pltpu.VMEM((peers, rank, q_cols), bf16),
            pltpu.VMEM((2 * rank, tokens), f32),
            pltpu.VMEM((2 * rank, tokens), f32),
            pltpu.VMEM((tokens, kv_cols), bf16),
            pltpu.VMEM((tokens, HEAD_DIM), bf16),
            dma((10,)),
            dma((PIECES,)),
            dma((PIECES,)),
            dma((parts + 2,)),
            dma((parts + 2,)),
            dma((parts + 2,)),
            dma((parts + 2,)),
            dma((parts + 2,)),
            dma((parts + 2,)),
            dma((peers,)),
            dma((peers,)),
            dma((parts + 2, peers)),
            dma((parts + 2, peers)),
            dma((1,)),
            dma((1,)),
            dma((len(GROUPS),)),
            dma((len(GROUPS),)),
        ],
        compiler_params=pltpu.CompilerParams(
            collective_id=0, has_side_effects=True, vmem_limit_bytes=60 * 1024 * 1024
        ),
        name="fused_attention",
    )(
        adapter_ids,
        adapter_slot,
        lengths,
        states,
        query_weight,
        key_value_weight,
        down_rows,
        query_up_store,
        key_value_store,
        trig,
    )


def solution(mesh):
    planes = mesh.shape["req"] // 4
    if mesh.shape["tp"] == 2 and planes == 4:
        body = functools.partial(local_fused, planes)
    else:
        body = local
    return jax.shard_map(
        body,
        mesh=mesh,
        in_specs=(
            P("req", "tp"),
            P(None, "tp"),
            P(None, "tp"),
            P("req"),
            P("req"),
            P(),
            P("req", "tp", None),
            P("req", None, "tp"),
            P("req", None, "tp"),
        ),
        out_specs=P("req", "tp"),
        check_vma=False,
    )
```

```python
import functools
import math

import jax
import jax.numpy as jnp
import numpy as np
from jax import lax
from jax.experimental import pallas as pl
from jax.experimental.pallas import tpu as pltpu
from jax.sharding import PartitionSpec as P

HEADS = 12
HEAD_DIM = 128


adapter_scale = 0.5
rope_base = 100000000000.0


def rotate(field):
    half = field.shape[-1] // 2
    count = field.shape[-3]
    position = jnp.arange(count).astype(jnp.float32)
    inverse = rope_base ** (-(jnp.arange(half).astype(jnp.float32) * 2.0) / field.shape[-1])
    angle = position[:, None] * inverse[None, :]
    cosine = jnp.cos(angle)[:, None, :]
    sine = jnp.sin(angle)[:, None, :]
    first_half = field[..., :half]
    second_half = field[..., half:]
    return jnp.concatenate(
        [first_half * cosine - second_half * sine, second_half * cosine + first_half * sine],
        axis=-1,
    )


def lookup_slots(wanted, adapter_slot):
    table = jnp.arange(adapter_slot.shape[0], dtype=jnp.int32)
    matches = wanted[:, None] == table[None, :]
    return jnp.sum(jnp.where(matches, adapter_slot[None, :], 0), axis=1)


def local(
    states,
    query_weight,
    key_value_weight,
    lengths,
    adapter_ids,
    adapter_slot,
    down_store,
    query_up_store,
    key_value_store,
):
    tp_index = lax.axis_index("tp")
    req_dev = lengths.shape[0]
    rows_total = states.shape[0]
    slot_len = rows_total // req_dev
    q_cols = query_weight.shape[1]
    kv_cols = key_value_weight.shape[1]
    heads_here = q_cols // HEAD_DIM
    pooled = (
        lax.all_gather(down_store, "req", axis=0, tiled=True),
        lax.all_gather(query_up_store, "req", axis=0, tiled=True),
        lax.all_gather(key_value_store, "req", axis=0, tiled=True),
    )
    own_slots = lookup_slots(adapter_ids, adapter_slot)
    adapter_down, adapter_query, adapter_pair = (
        jnp.take(member, own_slots, axis=0) for member in pooled
    )
    full_down = lax.all_gather(adapter_down, "tp", axis=1, tiled=True)
    piece = lax.all_gather(states, "tp", axis=1, tiled=True)
    width = piece.shape[1]
    grouped = piece.reshape(req_dev, slot_len, width)
    query_total = jnp.dot(piece, query_weight, preferred_element_type=jnp.float32)
    key_value_sum = jnp.dot(piece, key_value_weight, preferred_element_type=jnp.float32)
    rank_sum = jnp.einsum("rsd,rdk->rsk", grouped, full_down, preferred_element_type=jnp.float32)
    rank_mid = rank_sum.astype(jnp.bfloat16)
    rank_cols = rank_mid.shape[2] // 2
    query_addition = jnp.einsum(
        "rsk,rkc->rsc",
        rank_mid[:, :, :rank_cols],
        adapter_query,
        preferred_element_type=jnp.float32,
    ).reshape(rows_total, q_cols)
    key_value_extra = jnp.einsum(
        "rsk,rkc->rsc", rank_mid[:, :, rank_cols:], adapter_pair, preferred_element_type=jnp.float32
    ).reshape(rows_total, kv_cols)
    query_plain = query_total + adapter_scale * query_addition
    key_value_own = (key_value_sum + adapter_scale * key_value_extra).astype(jnp.bfloat16)
    pair_all = lax.all_gather(key_value_own, "tp", axis=1, tiled=True)
    key_width = pair_all.shape[1] // 2
    kv_heads = key_width // HEAD_DIM
    group = HEADS // kv_heads
    kv_index = tp_index * heads_here // group
    key_block = lax.dynamic_slice_in_dim(pair_all, kv_index * HEAD_DIM, HEAD_DIM, 1)
    value_block = lax.dynamic_slice_in_dim(pair_all, key_width + kv_index * HEAD_DIM, HEAD_DIM, 1)
    queries = rotate(query_plain.reshape(req_dev, slot_len, heads_here, HEAD_DIM)).astype(
        jnp.bfloat16
    )
    keys_one = rotate(key_block.astype(jnp.float32).reshape(req_dev, slot_len, 1, HEAD_DIM)).astype(
        jnp.bfloat16
    )[:, :, 0, :]
    values_one = value_block.reshape(req_dev, slot_len, HEAD_DIM)
    scale = 1.0 / math.sqrt(HEAD_DIM)
    scores = (
        jnp.einsum("rqhd,rkd->rhqk", queries, keys_one, preferred_element_type=jnp.float32) * scale
    )
    position = jnp.arange(slot_len, dtype=jnp.int32)
    allowed = (position[None, None, :] <= position[None, :, None]) & (
        position[None, None, :] < lengths[:, None, None]
    )
    scores = jnp.where(allowed[:, None, :, :], scores, -jnp.inf)
    highest = jnp.max(scores, axis=-1, keepdims=True)
    expo = jnp.exp(scores - highest)
    weights = (expo / jnp.sum(expo, axis=-1, keepdims=True)).astype(jnp.bfloat16)
    context = jnp.einsum("rhqk,rkd->rqhd", weights, values_one, preferred_element_type=jnp.float32)
    live_rows = position[None, :] < lengths[:, None]
    context = jnp.where(live_rows[:, :, None, None], context, 0.0)
    return context.reshape(rows_total, q_cols).astype(jnp.bfloat16)


MESH = pl.DeviceIdType.MESH
PIECES = 4
SENDS = 8
GROUPS = ((0, 192), (192, 64))


def fused(
    planes,
    ids,
    slots,
    lengths,
    states,
    wq,
    wkv,
    down_rows,
    query_rows,
    pair_rows,
    trig,
    out,
    own_st,
    other_st,
    wq_own,
    wkv_own,
    wq_other,
    wkv_other,
    total,
    plane_down,
    plane_q,
    plane_kv,
    turns,
    ids_own,
    ids_in,
    flags,
    leave_down,
    leave_kv,
    leave_q,
    land_down,
    land_kv,
    land_q,
    mid_out,
    mid_in,
    kv_own,
    kv_in,
    local_sem,
    st_send,
    st_recv,
    y_send,
    y_recv,
    c_send,
    c_recv,
    f_send,
    f_recv,
    i_send,
    i_recv,
    z_send,
    z_recv,
    m_send,
    m_recv,
    kv_send,
    kv_recv,
):
    r = lax.axis_index("req")
    tp = lax.axis_index("tp")
    per_plane = 4
    count = planes * per_plane
    half = own_st.shape[1]
    q_cols = wq.shape[1]
    tokens = own_st.shape[0]
    step = tokens // PIECES
    slab = tokens // SENDS
    parts = plane_down.shape[0]
    mine, rank = plane_q.shape[0] // per_plane, plane_q.shape[1]
    core_peer = r + 1 - 2 * (r % 2)
    y_peer = r + 2 - 4 * ((r // 2) % 2)
    z_peers = [(r + per_plane * d) % count for d in range(1, planes)]
    across = 1 - tp
    base = (r // per_plane) * (per_plane * mine)

    def place(index):
        return pl.ds((index % per_plane) * mine, mine)

    def remote(src, dst, send, recv, who):
        return pltpu.make_async_remote_copy(
            src_ref=src, dst_ref=dst, send_sem=send, recv_sem=recv, device_id=who, device_id_type=MESH
        )

    own_rows = pl.ds(pl.multiple_of(tp * half, half), half)
    other_rows = pl.ds(pl.multiple_of(across * half, half), half)
    loads = [
        pltpu.make_async_copy(states, own_st, local_sem.at[0]),
        pltpu.make_async_copy(wq.at[own_rows], wq_own, local_sem.at[1]),
        pltpu.make_async_copy(wkv.at[own_rows], wkv_own, local_sem.at[2]),
        pltpu.make_async_copy(wq.at[other_rows], wq_other, local_sem.at[3]),
        pltpu.make_async_copy(wkv.at[other_rows], wkv_other, local_sem.at[4]),
        pltpu.make_async_copy(trig, turns, local_sem.at[5]),
        pltpu.make_async_copy(query_rows, plane_q.at[place(r)], local_sem.at[6]),
        pltpu.make_async_copy(pair_rows, plane_kv.at[place(r)], local_sem.at[7]),
    ] + [
        pltpu.make_async_copy(
            down_rows.at[:, pl.ds(k * rank, rank)], plane_down.at[k, place(r)], local_sem.at[8 + k]
        )
        for k in range(parts)
    ]
    for copy in loads:
        copy.start()

    ids_own[...] = jnp.full(ids_own.shape, slots[ids[0]], jnp.int32)

    barrier = pltpu.get_barrier_semaphore()
    for peer in [core_peer, y_peer] + z_peers:
        pl.semaphore_signal(barrier, inc=1, device_id={"req": peer}, device_id_type=MESH)
    pl.semaphore_signal(barrier, inc=1, device_id={"tp": across}, device_id_type=MESH)
    for n in (0, 6, 7, 8, 9):
        loads[n].wait()
    pl.semaphore_wait(barrier, planes + 2)

    id_copies = [
        remote(ids_own, ids_in.at[d], i_send.at[d], i_recv.at[d], {"req": peer})
        for d, peer in enumerate(z_peers)
    ]
    st_copies = [
        remote(
            own_st.at[pl.ds(p * slab, slab)],
            other_st.at[pl.ds(p * slab, slab)],
            st_send.at[p],
            st_recv.at[p],
            {"tp": across},
        )
        for p in range(SENDS)
    ]
    def share(peer, send, recv):
        ends = [
            plane_down.at[k, place(r)] for k in range(parts)
        ] + [plane_kv.at[place(r)], plane_q.at[place(r)]]
        return [
            remote(block, block, send.at[n], recv.at[n], {"req": peer})
            for n, block in enumerate(ends)
        ]

    planes_of = [plane_down.at[k] for k in range(parts)] + [plane_kv, plane_q]
    leaves = [leave_down.at[k] for k in range(parts)] + [leave_kv, leave_q]
    lands = [land_down.at[k] for k in range(parts)] + [land_kv, land_q]
    y_copies = share(y_peer, y_send, y_recv)
    c_copies = share(core_peer, c_send, c_recv)
    f_copies = [
        remote(
            block.at[place(y_peer)],
            block.at[place(y_peer)],
            f_send.at[k],
            f_recv.at[k],
            {"req": core_peer},
        )
        for k, block in enumerate(planes_of)
    ]
    def after(done, following):
        done.wait_send()
        for copy in following:
            copy.start()

    for copy in [y_copies[0], st_copies[0]] + id_copies + [c_copies[0]] + st_copies[1:3]:
        copy.start()

    for n in (1, 2):
        loads[n].wait()
    total[:, :q_cols] = jnp.dot(own_st[...], wq_own[...], preferred_element_type=jnp.float32)
    total[:, q_cols:] = jnp.dot(own_st[...], wkv_own[...], preferred_element_type=jnp.float32)
    for n in (3, 4, 5):
        loads[n].wait()
    for copy in id_copies:
        copy.wait_recv()

    def add_q(p):
        span = pl.ds(p * step, step)
        total[span, :q_cols] += jnp.dot(
            other_st[span], wq_other[...], preferred_element_type=jnp.float32
        )

    def add_kv(p):
        span = pl.ds(p * step, step)
        total[span, q_cols:] += jnp.dot(
            other_st[span], wkv_other[...], preferred_element_type=jnp.float32
        )

    def arrived(p):
        for n in range(p * SENDS // PIECES, (p + 1) * SENDS // PIECES):
            st_copies[n].wait_recv()

    def add_piece(p):
        arrived(p)
        add_kv(p)
        add_q(p)

    z_copies = []

    for d in range(planes):
        wanted = ids_own[...] if d == 0 else ids_in[planes - 1 - d]
        for j in range(per_plane * mine):
            flags[d, j] = jnp.where(wanted == base + j, 1.0, 0.0).astype(jnp.bfloat16)

    def forward(k):
        y_copies[k].wait_recv()
        f_copies[k].start()

    def stage(k):
        c_copies[k].wait_recv()
        f_copies[k].wait_recv()
        source, leave, land = planes_of[k], leaves[k], lands[k]
        sums = [None] * planes
        for j in range(per_plane * mine):
            record = source[j]
            for d in range(planes):
                flag = jnp.concatenate([flags[d, j]] * (record.shape[1] // flags.shape[3]), axis=1)
                sums[d] = flag * record if j == 0 else sums[d] + flag * record
        for d in range(1, planes):
            leave[d - 1] = sums[d]
        sent = [
            remote(leave.at[d], land.at[d], z_send.at[k, d], z_recv.at[k, d], {"req": peer})
            for d, peer in enumerate(z_peers)
        ]
        for copy in sent:
            copy.start()
        z_copies.append(sent)
        return sums[0]

    def take(k):
        for copy in z_copies[k]:
            copy.wait_recv()
        record = held[k]
        for d in range(planes - 1):
            record = record + lands[k][d]
        return record

    def lower(k):
        mid_out[k * rank : (k + 1) * rank] = lax.dot_general(
            take(k), own_st[...], (((1,), (1,)), ((), ())), preferred_element_type=jnp.float32
        )

    held = []
    after(st_copies[0], [st_copies[3]])
    after(y_copies[0], [y_copies[1], c_copies[1]])
    forward(0)
    after(st_copies[1], [st_copies[4]])
    held.append(stage(0))
    add_piece(0)
    after(st_copies[2], [st_copies[5]])
    after(y_copies[1], y_copies[2:] + c_copies[2:])
    forward(1)
    after(st_copies[3], [st_copies[6]])
    held.append(stage(1))
    lower(0)
    add_piece(1)
    after(st_copies[4], [st_copies[7]])
    forward(2)
    forward(3)
    held.append(stage(2))
    held.append(stage(3))
    lower(1)
    mid_copy = remote(mid_out, mid_in, m_send.at[0], m_recv.at[0], {"tp": across})
    mid_copy.start()
    add_piece(2)
    mid_copy.wait_recv()
    mid = jnp.transpose(mid_out[...] + mid_in[...]).astype(jnp.bfloat16)
    total[:, q_cols:] += 0.5 * jnp.dot(mid[:, rank:], take(2), preferred_element_type=jnp.float32)

    keep = pl.ds(pl.multiple_of(tp * HEAD_DIM, HEAD_DIM), HEAD_DIM)
    give = pl.ds(pl.multiple_of(across * HEAD_DIM, HEAD_DIM), HEAD_DIM)
    scale = 1.0 / math.sqrt(HEAD_DIM)
    length = lengths[0]
    kv_copies = []
    key_parts = []
    value_parts = []

    def turn(x, span):
        return (x * turns[0, span] + pltpu.roll(x, HEAD_DIM // 2, 1) * turns[1, span]).astype(jnp.bfloat16)

    def swap(g):
        span = pl.ds(*GROUPS[g])
        kv_own[span] = total[span, q_cols:].astype(jnp.bfloat16)
        copy = remote(
            kv_own.at[span, give], kv_in.at[span], kv_send.at[g], kv_recv.at[g], {"tp": across}
        )
        copy.start()
        kv_copies.append(copy)

    def attend(g):
        first, size = GROUPS[g]
        span = pl.ds(first, size)
        turned = [
            turn(total[span, h * HEAD_DIM : (h + 1) * HEAD_DIM], span)
            for h in range(q_cols // HEAD_DIM)
        ]
        reach = first + size
        row = lax.broadcasted_iota(jnp.int32, (size, reach), 0) + first
        column = lax.broadcasted_iota(jnp.int32, (size, reach), 1)
        allowed = (column <= row) & (column < length)
        live = lax.broadcasted_iota(jnp.int32, (size, HEAD_DIM), 0) + first < length
        kv_copies[g].wait_recv()
        kept = kv_own[span, keep]
        came = kv_in[span]
        first_side = jnp.full(kept.shape, tp, jnp.int32) == 0
        key = jnp.where(first_side, kept.astype(jnp.float32), came.astype(jnp.float32))
        value = jnp.where(first_side, came.astype(jnp.float32), kept.astype(jnp.float32))
        key_parts.append(turn(key, span))
        value_parts.append(value.astype(jnp.bfloat16))
        keys = jnp.concatenate(key_parts, axis=0)
        values = jnp.concatenate(value_parts, axis=0)
        for h, query in enumerate(turned):
            scores = lax.dot_general(
                query, keys, (((1,), (1,)), ((), ())), preferred_element_type=jnp.float32
            )
            scores = jnp.where(allowed, scores * scale, -jnp.inf)
            expo = jnp.exp(scores - jnp.max(scores, axis=1, keepdims=True))
            share_of = 1.0 / jnp.sum(expo, axis=1, keepdims=True)
            weights = (expo * share_of).astype(jnp.bfloat16)
            mixed = jnp.dot(weights, values, preferred_element_type=jnp.float32)
            out[span, h * HEAD_DIM : (h + 1) * HEAD_DIM] = jnp.where(live, mixed, 0.0).astype(
                jnp.bfloat16
            )

    swap(0)
    total[:, :q_cols] += 0.5 * jnp.dot(
        mid[:, :rank], take(3), preferred_element_type=jnp.float32
    )
    arrived(PIECES - 1)
    add_kv(PIECES - 1)
    swap(1)
    add_q(PIECES - 1)
    attend(0)
    attend(1)

    for copy in id_copies + st_copies[5:] + y_copies[2:] + c_copies + f_copies + [mid_copy] + kv_copies:
        copy.wait_send()
    for sent in z_copies:
        for copy in sent:
            copy.wait_send()


def tables(tokens):
    half = HEAD_DIM // 2
    position = np.arange(tokens, dtype=np.float32)
    inverse = np.float32(rope_base) ** (-(np.arange(half, dtype=np.float32) * 2.0) / HEAD_DIM).astype(
        np.float32
    )
    angle = position[:, None] * inverse[None, :].astype(np.float32)
    cosine = np.cos(angle)
    sine = np.sin(angle)
    return np.stack(
        [np.concatenate([cosine, cosine], axis=1), np.concatenate([-sine, sine], axis=1)]
    ).astype(np.float32)


def local_fused(
    planes,
    states,
    query_weight,
    key_value_weight,
    lengths,
    adapter_ids,
    adapter_slot,
    down_store,
    query_up_store,
    key_value_store,
):
    tokens, half = states.shape
    q_cols = query_weight.shape[1]
    kv_cols = key_value_weight.shape[1]
    cols = q_cols + kv_cols
    mine, rank = query_up_store.shape[:2]
    down_rows = jnp.transpose(down_store, (0, 2, 1))
    parts = 2
    trig = tables(tokens)
    peers = planes - 1
    vmem = pl.BlockSpec(memory_space=pltpu.VMEM)
    smem = pl.BlockSpec(memory_space=pltpu.SMEM)
    hbm = pl.BlockSpec(memory_space=pl.ANY)
    bf16, f32 = jnp.bfloat16, jnp.float32
    dma = pltpu.SemaphoreType.DMA
    return pl.pallas_call(
        functools.partial(fused, planes),
        out_shape=jax.ShapeDtypeStruct((tokens, q_cols), bf16),
        in_specs=[smem] * 3 + [hbm] * 7,
        out_specs=vmem,
        scratch_shapes=[
            pltpu.VMEM((tokens, half), bf16),
            pltpu.VMEM((tokens, half), bf16),
            pltpu.VMEM((half, q_cols), bf16),
            pltpu.VMEM((half, kv_cols), bf16),
            pltpu.VMEM((half, q_cols), bf16),
            pltpu.VMEM((half, kv_cols), bf16),
            pltpu.VMEM((tokens, cols), f32),
            pltpu.VMEM((parts, 4 * mine, rank, half), bf16),
            pltpu.VMEM((4 * mine, rank, q_cols), bf16),
            pltpu.VMEM((4 * mine, rank, kv_cols), bf16),
            pltpu.VMEM(trig.shape, f32),
            pltpu.VMEM((16, 128), jnp.int32),
            pltpu.VMEM((peers, 16, 128), jnp.int32),
            pltpu.VMEM((planes, 4 * mine, 16, 128), bf16),
            pltpu.VMEM((parts, peers, rank, half), bf16),
            pltpu.VMEM((peers, rank, kv_cols), bf16),
            pltpu.VMEM((peers, rank, q_cols), bf16),
            pltpu.VMEM((parts, peers, rank, half), bf16),
            pltpu.VMEM((peers, rank, kv_cols), bf16),
            pltpu.VMEM((peers, rank, q_cols), bf16),
            pltpu.VMEM((2 * rank, tokens), f32),
            pltpu.VMEM((2 * rank, tokens), f32),
            pltpu.VMEM((tokens, kv_cols), bf16),
            pltpu.VMEM((tokens, HEAD_DIM), bf16),
            dma((10,)),
            dma((SENDS,)),
            dma((SENDS,)),
            dma((parts + 2,)),
            dma((parts + 2,)),
            dma((parts + 2,)),
            dma((parts + 2,)),
            dma((parts + 2,)),
            dma((parts + 2,)),
            dma((peers,)),
            dma((peers,)),
            dma((parts + 2, peers)),
            dma((parts + 2, peers)),
            dma((1,)),
            dma((1,)),
            dma((len(GROUPS),)),
            dma((len(GROUPS),)),
        ],
        compiler_params=pltpu.CompilerParams(
            collective_id=0, has_side_effects=True, vmem_limit_bytes=60 * 1024 * 1024
        ),
        name="fused_attention",
    )(
        adapter_ids,
        adapter_slot,
        lengths,
        states,
        query_weight,
        key_value_weight,
        down_rows,
        query_up_store,
        key_value_store,
        trig,
    )


def solution(mesh):
    planes = mesh.shape["req"] // 4
    if mesh.shape["tp"] == 2 and planes == 4:
        body = functools.partial(local_fused, planes)
    else:
        body = local
    return jax.shard_map(
        body,
        mesh=mesh,
        in_specs=(
            P("req", "tp"),
            P(None, "tp"),
            P(None, "tp"),
            P("req"),
            P("req"),
            P(),
            P("req", "tp", None),
            P("req", None, "tp"),
            P("req", None, "tp"),
        ),
        out_specs=P("req", "tp"),
        check_vma=False,
    )
```
